32 devices in a mesh: ctx: 4 (over y, x), mp: 8 (over z, core).
Axes of the slice: x: 2, y: 2, z: 4, core: 2. Of those that a mesh axis runs over, the one named last changes fastest.
Arguments:
- activations: bfloat16 [4096, 4096], P('ctx', 'mp'), may hold values from -36 to 36
- norm_gain: float32 [4096], P('mp'), may hold values from 0.1 to 1.9
- w_in: bfloat16 [4096, 3, 4096], P('ctx', None, 'mp'), may hold values from -0.09375 to 0.09375
- tail_rows: bfloat16 [3, 4096, 2], P(None, 'mp'), may hold values from -4 to 4
- short_filter: float32 [3, 3, 4096], P(None, None, 'mp'), may hold values from -3 to 3
- decay_rate: float32 [4096, 16], P('mp'), may hold values from 4.8828125e-05 to 0.08, as said below
- residue: float32 [4096, 16], P('mp'), may hold values from -1.5 to 1.5
- skip_gain: float32 [4096], P('mp'), may hold values from -4 to 4
- state_in: float32 [4096, 16], P('mp'), may hold values from -4 to 4
- w_out: bfloat16 [4096, 4096], P('mp', 'ctx'), may hold values from -0.125 to 0.125
Outputs:
- block_out: bfloat16 [4096, 4096], P('ctx', 'mp')
- state_out: float32 [4096, 16], P('mp')
The draws below stay inside these ranges and needn't reach their ends.
Inputs may be any that keep to these rules, and one draw needn't show every extreme that they name: `decay_rate`: every rate lies between 0.2/4096 and 0.08; any share of the modes may be slow (below 2/4096) or fast.
All inputs are finite; a program needn't handle non-finite values.
Results may differ from the reference program's by a relative error of at most 0.03.
Values may be sent and summed in bfloat16 or wider, within the bound.
No kernel may reach another device: no remote copies, remote signals or barrier semaphores. Data moves between devices by JAX's collectives and lax.ppermute only.
A program may use at most 128 MiB of HBM per device.

```python
import math
import jax
import jax.numpy as jnp
from jax import lax

D = 4096
ORDER = 16
TOKENS = 4096


def draw_activations(key, part):
    row_scale = jnp.exp(jax.random.uniform(jax.random.fold_in(key, 11), (TOKENS, 1), jnp.float32, math.log(0.3), math.log(3.0)))
    col_scale = jnp.exp(jax.random.uniform(jax.random.fold_in(key, 12), (1, D), jnp.float32, math.log(0.3), math.log(3.0)))
    base = jnp.clip(jax.random.normal(jax.random.fold_in(key, 15), (TOKENS, D), jnp.float32), -4.0, 4.0)
    return (base * row_scale * col_scale).astype(jnp.bfloat16)


def draw_decay_rate(key, part):
    lowest = 0.2 / TOKENS
    border = 2.0 / TOKENS
    highest_rate = 0.08
    chooser = jax.random.uniform(jax.random.fold_in(key, 21), (D, ORDER), jnp.float32)
    slow_rate = jnp.exp(jax.random.uniform(jax.random.fold_in(key, 22), (D, ORDER), jnp.float32, math.log(lowest), math.log(border)))
    fast_rate = jnp.exp(jax.random.uniform(jax.random.fold_in(key, 23), (D, ORDER), jnp.float32, math.log(border), math.log(highest_rate)))
    result = jnp.where(chooser < 0.5, slow_rate, fast_rate)
    return result.astype(jnp.float32)


def strengthened(values, own_key, source, target, blocks, factor):
    def block_of(axis_at):
        return (jnp.arange(values.shape[axis_at]) // (values.shape[axis_at] // blocks)).reshape((-1,) + (1,) * (values.ndim - 1 - axis_at))

    one_side = jax.random.permutation(own_key, blocks)[block_of(target)]
    other_side = (block_of(target) + blocks // 2) % blocks
    return jnp.where((block_of(source) == one_side) | (block_of(source) == other_side), factor * values, values)


def level_of(stream_key, dims, cuts, least, high):
    def one(axis_at, parts):
        heights = jax.random.uniform(jax.random.fold_in(jax.random.fold_in(stream_key, 6), axis_at), (parts,), jnp.float32, least / len(cuts), high / len(cuts))
        return jnp.repeat(jnp.exp(heights), dims[axis_at] // parts).reshape((-1,) + (1,) * (len(dims) - axis_at - 1))

    level = one(*cuts[0])
    for cut in cuts[1:]:
        level = level * one(*cut)
    return level


def scatter_about(own_key, dims, deviation, reach, split=(), held_as=jnp.bfloat16):
    values = jax.random.normal(own_key, dims, jnp.float32) * deviation
    if len(split) > 0:
        values = level_of(own_key, dims, split, -0.22, 0.18) * values
    return jnp.clip(values, min=-reach, max=reach).astype(held_as)


def noise_with(key, extent, deviation, most, cuts, heavy, kind=jnp.bfloat16):
    drawn = deviation * jax.random.normal(key, extent, jnp.float32)
    if cuts:
        drawn = drawn * level_of(key, extent, cuts, -0.22, 0.18)
    return jnp.clip(strengthened(drawn, jax.random.fold_in(key, 3), *heavy), -most, most).astype(kind)


def setup_inputs(seed: int = 0) -> dict:
    arg_keys = jax.random.split(jax.random.key(seed), 11)
    return {
        "activations": draw_activations(jax.random.fold_in(arg_keys[10], 71), 0),
        "norm_gain": jnp.clip(1.0 + 0.18 * jax.random.normal(arg_keys[1], (D,), jnp.float32), 0.1, 1.9),
        "w_in": scatter_about(arg_keys[2], (D, 3, D), D ** -0.5, 0.09375, ((0, 4), (2, 8))),
        "tail_rows": scatter_about(arg_keys[3], (3, D, 2), 1.0, 4.0, ((1, 8),)),
        "short_filter": scatter_about(arg_keys[4], (3, 3, D), 0.6, 3.0, ((2, 8),), jnp.float32),
        "decay_rate": draw_decay_rate(jax.random.fold_in(arg_keys[10], 71), 0),
        "residue": scatter_about(arg_keys[6], (D, ORDER), 0.25, 1.5, ((0, 8),), jnp.float32),
        "skip_gain": scatter_about(arg_keys[7], (D,), 1.0, 4.0, ((0, 8),), jnp.float32),
        "state_in": scatter_about(arg_keys[8], (D, ORDER), 1.0, 4.0, ((0, 8),), jnp.float32),
        "w_out": noise_with(arg_keys[9], (D, D), D ** -0.5, 0.125, ((0, 8), (1, 4)), (0, 1, 8, 2.0)),
    }


def reference(activations, norm_gain, w_in, tail_rows, short_filter, decay_rate, residue, skip_gain, state_in, w_out):
    act_float = activations.astype(jnp.float32)
    inverse = lax.rsqrt(lax.optimization_barrier(jnp.mean(act_float * act_float, axis=1, keepdims=True)) + 1e-06)
    normed = (act_float * inverse * norm_gain[None, :]).astype(jnp.bfloat16)
    model_width = activations.shape[1]
    flat = jnp.dot(normed, w_in.reshape(model_width, 3 * model_width), preferred_element_type=jnp.float32)
    projected = flat.astype(jnp.bfloat16).reshape(-1, 3, model_width).transpose(1, 2, 0)
    extended = jnp.concatenate([tail_rows, projected], axis=2).astype(jnp.float32)
    smoothed = short_filter[0][:, :, None] * extended[:, :, 2:]
    smoothed = smoothed + short_filter[1][:, :, None] * extended[:, :, 1:-1]
    smoothed = smoothed + short_filter[2][:, :, None] * extended[:, :, :-2]
    query = smoothed[0]
    mixed = (smoothed[1] * smoothed[2]).astype(jnp.bfloat16)
    mixed_float = mixed.astype(jnp.float32)
    decays = jnp.exp(-decay_rate)
    scales = jnp.sqrt(-jnp.expm1(-2.0 * decay_rate))

    def advance(state, column):
        state = decays * state + scales * column[:, None]
        return (state, lax.optimization_barrier(jnp.sum(residue * state, axis=1)))
    state_out, outputs = lax.scan(advance, state_in, mixed_float.T)
    response = outputs.T + skip_gain[:, None] * mixed_float
    gated = (query * response).astype(jnp.bfloat16)
    branch = jnp.dot(gated.T, w_out, preferred_element_type=jnp.float32)
    return ((act_float + branch).astype(jnp.bfloat16), state_out)
```

```python
import functools

import jax
import jax.numpy as jnp
from jax import lax
from jax.experimental import pallas as pl
from jax.experimental.pallas import tpu as pltpu
from jax.sharding import PartitionSpec as P

LANES = 128
SEGMENTS = 8
f32 = jnp.float32
bf16 = jnp.bfloat16


def swap_route(size, bit):
    return [(i, i ^ bit) for i in range(size)]


def gathered_blocks(block):
    size = lax.axis_size("ctx")
    me = lax.axis_index("ctx")
    rows = block.shape[0]
    if size != 4:
        whole = lax.all_gather(block, "ctx", axis=0)
        return [(i, 0, whole[i]) for i in range(size)]
    half = rows // 2
    by_x = lax.ppermute(block, "ctx", swap_route(size, 1))
    by_y = lax.ppermute(block, "ctx", swap_route(size, 2))
    far_top = lax.ppermute(by_y[:half], "ctx", swap_route(size, 1))
    far_bottom = lax.ppermute(by_x[half:], "ctx", swap_route(size, 2))
    return [
        (me, 0, block),
        (me ^ 1, 0, by_x),
        (me ^ 2, 0, by_y),
        (me ^ 3, 0, far_top),
        (me ^ 3, half, far_bottom),
    ]


def shifted_start(ref, tail_ref, back, segment):
    last = ref[pl.ds(segment - back, SEGMENTS, stride=segment), :]
    rolled = pltpu.roll(last, 1, 0)
    first = lax.broadcasted_iota(jnp.int32, rolled.shape, 0) == 0
    return jnp.where(first, jnp.broadcast_to(tail_ref[2 - back : 3 - back, :], rolled.shape), rolled)


def wide(row):
    return jnp.broadcast_to(row, (SEGMENTS, row.shape[1]))


def local_kernel(
    segment, modes, k_ref, v_ref, tail_k_ref, tail_v_ref, taps_k_ref, taps_v_ref, lam_ref, weight_ref,
    scale_ref, skip_ref, reach_ref, resp_ref, ends_ref, last_ref,
):
    lam = [wide(lam_ref[n : n + 1, :]) for n in range(modes)]
    weight = [wide(weight_ref[n : n + 1, :]) for n in range(modes)]
    tk = [wide(taps_k_ref[i : i + 1, :]) for i in range(3)]
    tv = [wide(taps_v_ref[i : i + 1, :]) for i in range(3)]
    skip = wide(skip_ref[...])
    zero = jnp.zeros((SEGMENTS, LANES), f32)

    def step(t, carry):
        k1, k2, v1, v2, state = carry
        at = pl.ds(t, SEGMENTS, stride=segment)
        k = k_ref[at, :]
        v = v_ref[at, :]
        u = (tk[0] * k + tk[1] * k1 + tk[2] * k2) * (tv[0] * v + tv[1] * v1 + tv[2] * v2)
        sums = [skip * u, zero, zero, zero]
        moved = []
        for n in range(modes):
            s = lam[n] * state[n] + u
            moved.append(s)
            sums[n % 4] = sums[n % 4] + weight[n] * s
        resp_ref[at, :] = (sums[0] + sums[1]) + (sums[2] + sums[3])
        return (k, k1, v, v1, tuple(moved))

    carry = (
        shifted_start(k_ref, tail_k_ref, 1, segment),
        shifted_start(k_ref, tail_k_ref, 2, segment),
        shifted_start(v_ref, tail_v_ref, 1, segment),
        shifted_start(v_ref, tail_v_ref, 2, segment),
        (zero,) * modes,
    )
    state = lax.fori_loop(0, segment, step, carry, unroll=4)[4]
    for n in range(modes):
        end = wide(scale_ref[n : n + 1, :]) * state[n]
        rows = slice(n * SEGMENTS, (n + 1) * SEGMENTS)
        ends_ref[rows, :] = end
        last_ref[n : n + 1, :] = jnp.sum(end * reach_ref[rows, :], axis=0, keepdims=True)


def gate_kernel(
    segment, modes, parts, q_ref, tail_q_ref, taps_q_ref, lam_ref, hop_ref, residue_ref, resp_ref, ends_ref,
    states_ref, shares_ref, gated_ref, enter_ref, wide_ref,
):
    now = shares_ref[0:modes, :] * states_ref[0:modes, :]
    for i in range(1, parts):
        rows = slice(i * modes, (i + 1) * modes)
        now = now + shares_ref[rows, :] * states_ref[rows, :]
    hop = hop_ref[...]
    for s in range(SEGMENTS):
        at = pl.ds(s, modes, stride=SEGMENTS)
        enter_ref[at, :] = now
        now = hop * now + ends_ref[at, :]
    lam = [wide(lam_ref[n : n + 1, :]) for n in range(modes)]
    taps = [wide(taps_q_ref[i : i + 1, :]) for i in range(3)]
    carried = tuple(
        wide(residue_ref[n : n + 1, :]) * lam[n] * enter_ref[n * SEGMENTS : (n + 1) * SEGMENTS, :]
        for n in range(modes)
    )

    def step(t, carry):
        q1, q2, carried = carry
        at = pl.ds(t, SEGMENTS, stride=segment)
        q = q_ref[at, :]
        sums = [resp_ref[at, :], carried[0], carried[1], carried[2]]
        for n in range(3, modes):
            sums[n % 4] = sums[n % 4] + carried[n]
        response = (sums[0] + sums[1]) + (sums[2] + sums[3])
        wide_ref[at, :] = (taps[0] * q + taps[1] * q1 + taps[2] * q2) * response
        return (q, q1, tuple(lam[n] * carried[n] for n in range(modes)))

    start = (shifted_start(q_ref, tail_q_ref, 1, segment), shifted_start(q_ref, tail_q_ref, 2, segment), carried)
    lax.fori_loop(0, segment, step, start, unroll=4)
    gated_ref[...] = wide_ref[...].astype(gated_ref.dtype)


def column(rows, first):
    return pl.BlockSpec((rows, LANES), lambda c: (0, first + c))


def local_filter(projected, tails, taps, tables):
    tokens, width = projected.shape
    blocks = width // 3 // LANES
    modes = tables["lam"].shape[0]
    flops = tokens * width // 3 * modes * 4
    return pl.pallas_call(
        functools.partial(local_kernel, tokens // SEGMENTS, modes),
        grid=(blocks,),
        in_specs=[
            column(tokens, blocks),
            column(tokens, 2 * blocks),
            column(2, blocks),
            column(2, 2 * blocks),
            column(3, blocks),
            column(3, 2 * blocks),
            column(modes, 0),
            column(modes, 0),
            column(modes, 0),
            column(1, 0),
            column(modes * SEGMENTS, 0),
        ],
        out_specs=[column(tokens, 0), column(modes * SEGMENTS, 0), column(modes, 0)],
        out_shape=[
            jax.ShapeDtypeStruct((tokens, width // 3), f32),
            jax.ShapeDtypeStruct((modes * SEGMENTS, width // 3), f32),
            jax.ShapeDtypeStruct((modes, width // 3), f32),
        ],
        cost_estimate=pl.CostEstimate(flops=flops, bytes_accessed=tokens * width * 4, transcendentals=0),
        compiler_params=pltpu.CompilerParams(vmem_limit_bytes=32 * 2**20),
        name="local_filter",
    )(
        projected, projected, tails, tails, taps, taps, tables["lam"], tables["weight"], tables["scale"],
        tables["skip"], tables["reach"],
    )


def gated_signal(projected, tails, taps, tables, response, ends, states):
    tokens, width = projected.shape
    blocks = width // 3 // LANES
    modes = tables["lam"].shape[0]
    parts = states.shape[0] // modes
    flops = tokens * width // 3 * modes * 2
    return pl.pallas_call(
        functools.partial(gate_kernel, tokens // SEGMENTS, modes, parts),
        grid=(blocks,),
        in_specs=[
            column(tokens, 0),
            column(2, 0),
            column(3, 0),
            column(modes, 0),
            column(modes, 0),
            column(modes, 0),
            column(tokens, 0),
            column(modes * SEGMENTS, 0),
            column(parts * modes, 0),
            column(parts * modes, 0),
        ],
        out_specs=column(tokens, 0),
        out_shape=jax.ShapeDtypeStruct((tokens, width // 3), bf16),
        scratch_shapes=[pltpu.VMEM((modes * SEGMENTS, LANES), f32), pltpu.VMEM((tokens, LANES), f32)],
        cost_estimate=pl.CostEstimate(flops=flops, bytes_accessed=tokens * width * 3, transcendentals=0),
        compiler_params=pltpu.CompilerParams(vmem_limit_bytes=32 * 2**20),
        name="gated_signal",
    )(
        projected, tails, taps, tables["lam"], tables["hop"], tables["residue"], response, ends, states,
        tables["shares"],
    )


def filter_tables(decay_rate, residue, skip_gain, tokens):
    me = lax.axis_index("ctx")
    size = lax.axis_size("ctx")
    rate = decay_rate.T
    modes, channels = rate.shape
    scale = jnp.sqrt(-jnp.expm1(-2.0 * rate))
    segment = tokens // SEGMENTS
    ahead = (SEGMENTS - 1 - jnp.arange(SEGMENTS, dtype=f32)) * segment
    reach = jnp.exp(-rate[:, None, :] * ahead[None, :, None]).reshape(modes * SEGMENTS, channels)
    index = jnp.arange(size)
    gap = (me - 1 - index).astype(f32) * tokens
    shares = jnp.where(
        (index < me)[:, None, None], jnp.exp(-rate[None] * jnp.maximum(gap, 0.0)[:, None, None]), 0.0
    )
    first = jnp.exp(-rate * (me * tokens).astype(f32))[None]
    final_gap = (size - 1 - index).astype(f32) * tokens
    final = jnp.exp(-rate[None] * final_gap[:, None, None])
    final_first = jnp.exp(-rate * (size * tokens))[None]
    return {
        "lam": jnp.exp(-rate),
        "hop": jnp.exp(-rate * segment),
        "weight": residue.T * scale,
        "residue": residue.T,
        "scale": scale,
        "skip": skip_gain[None, :],
        "reach": reach,
        "shares": jnp.concatenate([shares, first]).reshape((size + 1) * modes, channels),
        "final": jnp.concatenate([final, final_first]),
    }


def cut(tables, start, stop):
    return {name: table[..., start:stop] for name, table in tables.items()}


def local(
    activations,
    norm_gain,
    w_in,
    tail_rows,
    short_filter,
    decay_rate,
    residue,
    skip_gain,
    state_in,
    w_out,
):
    tokens, features = activations.shape
    channels = w_in.shape[2]
    mp = lax.axis_size("mp")
    ctx = lax.axis_size("ctx")
    me = lax.axis_index("ctx")
    model_width = features * mp
    groups = 2 if channels % (2 * LANES) == 0 else 1
    share = channels // groups
    act_float = activations.astype(f32)
    scaled = (act_float * norm_gain[None, :]).astype(bf16)
    everything = lax.all_gather(scaled, "mp", axis=0)
    squares = lax.psum(jnp.sum(act_float * act_float, axis=1), "mp")
    inverse = lax.rsqrt(squares / model_width + 1e-06)[:, None]
    per_block = mp // ctx
    by_block = everything.reshape(ctx, per_block, tokens, features)

    def project(blocks):
        total = None
        for owner, first, rows in blocks:
            for i in range(0, rows.shape[0], features):
                source = lax.dynamic_index_in_dim(by_block, owner, 0, False)[(first + i) // features]
                part = lax.dot_general(
                    source, rows[i : i + features], (((1,), (0,)), ((), ())), preferred_element_type=f32
                )
                total = part if total is None else total + part
        return total * inverse

    tables = filter_tables(decay_rate, residue, skip_gain, tokens)
    start_state = state_in.T
    taps_all = short_filter
    tails_all = tail_rows.transpose(2, 0, 1).astype(f32)
    pieces = [w_in[:, :, g * share : (g + 1) * share].reshape(-1, 3 * share) for g in range(groups)]
    arriving = [gathered_blocks(piece) for piece in pieces]
    outputs = []
    finals = []
    for g in range(groups):
        span = slice(g * share, (g + 1) * share)
        own = cut(tables, g * share, (g + 1) * share)
        taps = taps_all[:, :, span].reshape(3, 3 * share)
        projected = project(arriving[g])
        behind = lax.ppermute(projected[-2:], "ctx", [(i, i + 1) for i in range(ctx - 1)])
        tails = jnp.where(me == 0, tails_all[:, :, span].reshape(2, 3 * share), behind)
        response, ends, last = local_filter(projected, tails, taps, own)
        lasts = lax.all_gather(last, "ctx", axis=0)
        states = jnp.concatenate([lasts, start_state[None, :, span]])
        finals.append(jnp.sum(own["final"] * states, axis=0))
        outputs.append(
            gated_signal(projected, tails, taps, own, response, ends, states.reshape(-1, share))
        )
    state_out = jnp.concatenate(finals, axis=1).T
    gated = jnp.concatenate(outputs, axis=1)
    panel = lax.all_gather(w_out, "ctx", axis=1, tiled=True)
    partial = lax.dot_general(panel, gated, (((0,), (1,)), ((), ())), preferred_element_type=f32)
    branch = lax.psum_scatter(partial.astype(bf16), "mp", scatter_dimension=0, tiled=True).astype(f32).T
    return ((act_float + branch).astype(bf16), state_out)


def solution(mesh):
    placed = (
        P("ctx", "mp"),
        P("mp"),
        P("ctx", None, "mp"),
        P(None, "mp", None),
        P(None, None, "mp"),
        P("mp", None),
        P("mp", None),
        P("mp"),
        P("mp", None),
        P("mp", "ctx"),
    )
    return jax.shard_map(
        local,
        mesh=mesh,
        in_specs=placed,
        out_specs=(P("ctx", "mp"), P("mp", None)),
        check_vma=False,
    )
```

```python
import functools
import math

import jax
import jax.numpy as jnp
from jax import lax
from jax.experimental import pallas as pl
from jax.experimental.pallas import tpu as pltpu
from jax.sharding import PartitionSpec as P

LANES = 128
SEGMENTS = 8
f32 = jnp.float32
bf16 = jnp.bfloat16


def swap_route(size, bit):
    return [(i, i ^ bit) for i in range(size)]


def gathered_blocks(block):
    size = lax.axis_size("ctx")
    me = lax.axis_index("ctx")
    rows = block.shape[0]
    if size != 4:
        whole = lax.all_gather(block, "ctx", axis=0)
        return [(i, 0, whole[i]) for i in range(size)]
    half = rows // 2
    by_x = lax.ppermute(block, "ctx", swap_route(size, 1))
    by_y = lax.ppermute(block, "ctx", swap_route(size, 2))
    far_top = lax.ppermute(by_y[:half], "ctx", swap_route(size, 1))
    far_bottom = lax.ppermute(by_x[half:], "ctx", swap_route(size, 2))
    return [
        (me, 0, block),
        (me ^ 1, 0, by_x),
        (me ^ 2, 0, by_y),
        (me ^ 3, 0, far_top),
        (me ^ 3, half, far_bottom),
    ]


def shifted_start(ref, tail_ref, back, segment):
    last = ref[pl.ds(segment - back, SEGMENTS, stride=segment), :]
    rolled = pltpu.roll(last, 1, 0)
    first = lax.broadcasted_iota(jnp.int32, rolled.shape, 0) == 0
    return jnp.where(first, jnp.broadcast_to(tail_ref[2 - back : 3 - back, :], rolled.shape), rolled)


def wide(row):
    return jnp.broadcast_to(row, (SEGMENTS, row.shape[1]))


def local_kernel(
    segment, modes, k_ref, v_ref, tail_k_ref, tail_v_ref, taps_k_ref, taps_v_ref, lam_ref, weight_ref,
    scale_ref, skip_ref, reach_ref, resp_ref, ends_ref, last_ref,
):
    lam = [wide(lam_ref[n : n + 1, :]) for n in range(modes)]
    weight = [wide(weight_ref[n : n + 1, :]) for n in range(modes)]
    tk = [wide(taps_k_ref[i : i + 1, :]) for i in range(3)]
    tv = [wide(taps_v_ref[i : i + 1, :]) for i in range(3)]
    skip = wide(skip_ref[...])
    zero = jnp.zeros((SEGMENTS, LANES), f32)

    def step(t, carry):
        k1, k2, v1, v2, state = carry
        at = pl.ds(t, SEGMENTS, stride=segment)
        k = k_ref[at, :]
        v = v_ref[at, :]
        u = (tk[0] * k + tk[1] * k1 + tk[2] * k2) * (tv[0] * v + tv[1] * v1 + tv[2] * v2)
        sums = [skip * u, zero, zero, zero]
        moved = []
        for n in range(modes):
            s = lam[n] * state[n] + u
            moved.append(s)
            sums[n % 4] = sums[n % 4] + weight[n] * s
        resp_ref[at, :] = (sums[0] + sums[1]) + (sums[2] + sums[3])
        return (k, k1, v, v1, tuple(moved))

    carry = (
        shifted_start(k_ref, tail_k_ref, 1, segment),
        shifted_start(k_ref, tail_k_ref, 2, segment),
        shifted_start(v_ref, tail_v_ref, 1, segment),
        shifted_start(v_ref, tail_v_ref, 2, segment),
        (zero,) * modes,
    )
    state = lax.fori_loop(0, segment, step, carry, unroll=4)[4]
    for n in range(modes):
        end = wide(scale_ref[n : n + 1, :]) * state[n]
        rows = slice(n * SEGMENTS, (n + 1) * SEGMENTS)
        ends_ref[rows, :] = end
        last_ref[n : n + 1, :] = jnp.sum(end * reach_ref[rows, :], axis=0, keepdims=True)


def gate_kernel(
    segment, modes, parts, q_ref, tail_q_ref, taps_q_ref, lam_ref, hop_ref, residue_ref, resp_ref, ends_ref,
    states_ref, shares_ref, gated_ref, enter_ref, wide_ref,
):
    now = shares_ref[0:modes, :] * states_ref[0:modes, :]
    for i in range(1, parts):
        rows = slice(i * modes, (i + 1) * modes)
        now = now + shares_ref[rows, :] * states_ref[rows, :]
    hop = hop_ref[...]
    for s in range(SEGMENTS):
        at = pl.ds(s, modes, stride=SEGMENTS)
        enter_ref[at, :] = now
        now = hop * now + ends_ref[at, :]
    lam = [wide(lam_ref[n : n + 1, :]) for n in range(modes)]
    taps = [wide(taps_q_ref[i : i + 1, :]) for i in range(3)]
    carried = tuple(
        wide(residue_ref[n : n + 1, :]) * lam[n] * enter_ref[n * SEGMENTS : (n + 1) * SEGMENTS, :]
        for n in range(modes)
    )

    def step(t, carry):
        q1, q2, carried = carry
        at = pl.ds(t, SEGMENTS, stride=segment)
        q = q_ref[at, :]
        sums = [resp_ref[at, :], carried[0], carried[1], carried[2]]
        for n in range(3, modes):
            sums[n % 4] = sums[n % 4] + carried[n]
        response = (sums[0] + sums[1]) + (sums[2] + sums[3])
        wide_ref[at, :] = (taps[0] * q + taps[1] * q1 + taps[2] * q2) * response
        return (q, q1, tuple(lam[n] * carried[n] for n in range(modes)))

    start = (shifted_start(q_ref, tail_q_ref, 1, segment), shifted_start(q_ref, tail_q_ref, 2, segment), carried)
    lax.fori_loop(0, segment, step, start, unroll=4)
    gated_ref[...] = wide_ref[...].astype(gated_ref.dtype)


def column(rows, first):
    return pl.BlockSpec((rows, LANES), lambda c: (0, first + c))


def local_filter(projected, tails, taps, tables):
    tokens, width = projected.shape
    blocks = width // 3 // LANES
    modes = tables["lam"].shape[0]
    flops = tokens * width // 3 * modes * 4
    return pl.pallas_call(
        functools.partial(local_kernel, tokens // SEGMENTS, modes),
        grid=(blocks,),
        in_specs=[
            column(tokens, blocks),
            column(tokens, 2 * blocks),
            column(2, blocks),
            column(2, 2 * blocks),
            column(3, blocks),
            column(3, 2 * blocks),
            column(modes, 0),
            column(modes, 0),
            column(modes, 0),
            column(1, 0),
            column(modes * SEGMENTS, 0),
        ],
        out_specs=[column(tokens, 0), column(modes * SEGMENTS, 0), column(modes, 0)],
        out_shape=[
            jax.ShapeDtypeStruct((tokens, width // 3), f32),
            jax.ShapeDtypeStruct((modes * SEGMENTS, width // 3), f32),
            jax.ShapeDtypeStruct((modes, width // 3), f32),
        ],
        cost_estimate=pl.CostEstimate(flops=flops, bytes_accessed=tokens * width * 4, transcendentals=0),
        compiler_params=pltpu.CompilerParams(vmem_limit_bytes=32 * 2**20),
        name="local_filter",
    )(
        projected, projected, tails, tails, taps, taps, tables["lam"], tables["weight"], tables["scale"],
        tables["skip"], tables["reach"],
    )


def gated_signal(projected, tails, taps, tables, response, ends, states):
    tokens, width = projected.shape
    blocks = width // 3 // LANES
    modes = tables["lam"].shape[0]
    parts = states.shape[0] // modes
    flops = tokens * width // 3 * modes * 2
    return pl.pallas_call(
        functools.partial(gate_kernel, tokens // SEGMENTS, modes, parts),
        grid=(blocks,),
        in_specs=[
            column(tokens, 0),
            column(2, 0),
            column(3, 0),
            column(modes, 0),
            column(modes, 0),
            column(modes, 0),
            column(tokens, 0),
            column(modes * SEGMENTS, 0),
            column(parts * modes, 0),
            column(parts * modes, 0),
        ],
        out_specs=column(tokens, 0),
        out_shape=jax.ShapeDtypeStruct((tokens, width // 3), bf16),
        scratch_shapes=[pltpu.VMEM((modes * SEGMENTS, LANES), f32), pltpu.VMEM((tokens, LANES), f32)],
        cost_estimate=pl.CostEstimate(flops=flops, bytes_accessed=tokens * width * 3, transcendentals=0),
        compiler_params=pltpu.CompilerParams(vmem_limit_bytes=32 * 2**20),
        name="gated_signal",
    )(
        projected, tails, taps, tables["lam"], tables["hop"], tables["residue"], response, ends, states,
        tables["shares"],
    )


def project_kernel(chunks, order_ref, all_ref, *refs):
    pieces, inverse_ref, out_ref = refs[:-2], refs[-2], refs[-1]
    features = all_ref.shape[2]
    total = None
    for n, (piece, first) in enumerate(chunks):
        part = jnp.dot(
            all_ref[order_ref[n]], pieces[piece][first : first + features, :], preferred_element_type=f32
        )
        total = part if total is None else total + part
    out_ref[...] = total * inverse_ref[...]


def project(everything, blocks, inverse):
    mp, tokens, features = everything.shape
    per_block = mp // lax.axis_size("ctx")
    width = blocks[0][2].shape[1]
    chunks, order = [], []
    for n, (owner, first, rows) in enumerate(blocks):
        for i in range(0, rows.shape[0], features):
            chunks.append((n, i))
            order.append(owner * per_block + (first + i) // features)
    tile = math.gcd(tokens, 256)
    whole = [pl.BlockSpec(rows.shape, lambda m, order: (0, 0)) for _, _, rows in blocks]
    return pl.pallas_call(
        functools.partial(project_kernel, chunks),
        grid_spec=pltpu.PrefetchScalarGridSpec(
            num_scalar_prefetch=1,
            grid=(tokens // tile,),
            in_specs=[
                pl.BlockSpec((mp, tile, features), lambda m, order: (0, m, 0)),
                *whole,
                pl.BlockSpec((tile, 1), lambda m, order: (m, 0)),
            ],
            out_specs=pl.BlockSpec((tile, width), lambda m, order: (m, 0)),
        ),
        out_shape=jax.ShapeDtypeStruct((tokens, width), f32),
        cost_estimate=pl.CostEstimate(
            flops=2 * tokens * width * mp * features, bytes_accessed=2 * mp * features * (tokens + width), transcendentals=0
        ),
        compiler_params=pltpu.CompilerParams(vmem_limit_bytes=40 * 2**20),
        name="project",
    )(jnp.stack([jnp.asarray(o, jnp.int32) for o in order]), everything, *[rows for _, _, rows in blocks], inverse)


def output_kernel(order_ref, gated_ref, panel_ref, base_ref, out_ref):
    total = base_ref[...].astype(f32)
    for x in range(panel_ref.shape[0]):
        total = total + jnp.dot(gated_ref[order_ref[x]], panel_ref[x], preferred_element_type=f32)
    out_ref[...] = total.astype(out_ref.dtype)


def add_outputs(gated, panel, group, order, base, dtype):
    mp, tokens, share = gated.shape
    columns = panel.shape[2]
    tile = math.gcd(tokens, 256)
    return pl.pallas_call(
        output_kernel,
        grid_spec=pltpu.PrefetchScalarGridSpec(
            num_scalar_prefetch=1,
            grid=(tokens // tile,),
            in_specs=[
                pl.BlockSpec((mp, tile, share), lambda m, order: (0, m, 0)),
                pl.BlockSpec((mp, share, columns), lambda m, order: (0, group, 0)),
                pl.BlockSpec((tile, columns), lambda m, order: (m, 0)),
            ],
            out_specs=pl.BlockSpec((tile, columns), lambda m, order: (m, 0)),
        ),
        out_shape=jax.ShapeDtypeStruct((tokens, columns), dtype),
        cost_estimate=pl.CostEstimate(
            flops=2 * tokens * columns * mp * share, bytes_accessed=2 * mp * share * (tokens + columns), transcendentals=0
        ),
        compiler_params=pltpu.CompilerParams(vmem_limit_bytes=40 * 2**20),
        name="add_outputs",
    )(order, gated, panel, base)


def exchange(rows, axis, masks):
    size = lax.axis_size(axis)
    return [
        rows[n] if mask == 0 else lax.ppermute(rows[n], axis, swap_route(size, mask)) for n, mask in enumerate(masks)
    ]


def output_panel(w_out, after):
    channels, wide_columns = w_out.shape
    ctx, mp = lax.axis_size("ctx"), lax.axis_size("mp")
    me, place = lax.axis_index("ctx"), lax.axis_index("mp")
    part, per = channels // ctx, mp // ctx
    columns = wide_columns // per
    if (ctx, mp) != (4, 8):
        rows = lax.all_to_all(w_out.reshape(ctx, part, wide_columns), "ctx", 0, 0)
        rows = rows.reshape(ctx, part, per, columns).swapaxes(1, 2).reshape(mp, part, columns)
        rows = lax.all_to_all(rows, "mp", 0, 0)
        panel = lax.all_gather(rows, "ctx", axis=1).reshape(mp, channels, columns)
        return panel, jnp.arange(mp, dtype=jnp.int32)
    mine = w_out.reshape(ctx, part, wide_columns)
    sent = [lax.dynamic_index_in_dim(mine, me ^ d, 0, False) for d in range(ctx)]
    by_owner = jnp.stack(exchange(sent, "ctx", range(ctx)))
    by_owner = lax.optimization_barrier((by_owner, after))[0]
    chip, core = place // per, place % per
    sent = [lax.dynamic_index_in_dim(by_owner, (chip ^ d) ^ me, 0, False) for d in range(mp // per)]
    rows = jnp.stack(exchange(sent, "mp", range(0, mp, per)))
    keep = lax.dynamic_slice_in_dim(rows, core * columns, columns, 2)
    give = lax.dynamic_slice_in_dim(rows, (core ^ 1) * columns, columns, 2)
    rows = jnp.stack([keep, lax.ppermute(give, "mp", swap_route(mp, 1))], axis=1).reshape(mp, 1, part, columns)
    panel = jnp.zeros((mp, ctx, part, columns), w_out.dtype)
    for owner, first, block in gathered_blocks(rows):
        panel = lax.dynamic_update_slice(panel, block, (first, owner, 0, 0))
    return panel.reshape(mp, channels, columns), place ^ jnp.arange(mp, dtype=jnp.int32)


def end_states(last):
    size = lax.axis_size("ctx")
    if size != 4:
        return lax.all_gather(last, "ctx", axis=0)
    return jnp.stack(exchange([last] * size, "ctx", range(size)))


def ctx_order():
    size = lax.axis_size("ctx")
    return lax.axis_index("ctx") ^ jnp.arange(size) if size == 4 else jnp.arange(size)


def filter_tables(decay_rate, residue, skip_gain, tokens):
    me = lax.axis_index("ctx")
    size = lax.axis_size("ctx")
    rate = decay_rate.T
    modes, channels = rate.shape
    scale = jnp.sqrt(-jnp.expm1(-2.0 * rate))
    segment = tokens // SEGMENTS
    ahead = (SEGMENTS - 1 - jnp.arange(SEGMENTS, dtype=f32)) * segment
    reach = jnp.exp(-rate[:, None, :] * ahead[None, :, None]).reshape(modes * SEGMENTS, channels)
    index = ctx_order()
    gap = (me - 1 - index).astype(f32) * tokens
    shares = jnp.where(
        (index < me)[:, None, None], jnp.exp(-rate[None] * jnp.maximum(gap, 0.0)[:, None, None]), 0.0
    )
    first = jnp.exp(-rate * (me * tokens).astype(f32))[None]
    final_gap = (size - 1 - index).astype(f32) * tokens
    final = jnp.exp(-rate[None] * final_gap[:, None, None])
    final_first = jnp.exp(-rate * (size * tokens))[None]
    return {
        "lam": jnp.exp(-rate),
        "hop": jnp.exp(-rate * segment),
        "weight": residue.T * scale,
        "residue": residue.T,
        "scale": scale,
        "skip": skip_gain[None, :],
        "reach": reach,
        "shares": jnp.concatenate([shares, first]).reshape((size + 1) * modes, channels),
        "final": jnp.concatenate([final, final_first]),
    }


def cut(tables, start, stop):
    return {name: table[..., start:stop] for name, table in tables.items()}


def local(
    activations,
    norm_gain,
    w_in,
    tail_rows,
    short_filter,
    decay_rate,
    residue,
    skip_gain,
    state_in,
    w_out,
):
    tokens, features = activations.shape
    channels = w_in.shape[2]
    mp = lax.axis_size("mp")
    ctx = lax.axis_size("ctx")
    me = lax.axis_index("ctx")
    model_width = features * mp
    groups = 2 if channels % (2 * LANES) == 0 else 1
    share = channels // groups
    act_float = activations.astype(f32)
    scaled = (act_float * norm_gain[None, :]).astype(bf16)
    everything = lax.all_gather(scaled, "mp", axis=0)
    squares = lax.psum(jnp.sum(act_float * act_float, axis=1), "mp")
    inverse = lax.rsqrt(squares / model_width + 1e-06)[:, None]
    tables = filter_tables(decay_rate, residue, skip_gain, tokens)
    start_state = state_in.T
    taps_all = short_filter
    tails_all = tail_rows.transpose(2, 0, 1).astype(f32)
    pieces = [w_in[:, :, g * share : (g + 1) * share].reshape(-1, 3 * share) for g in range(groups)]
    arriving = [gathered_blocks(piece) for piece in pieces]
    panel, order = output_panel(w_out, everything[0, :16, :LANES])
    total = activations
    finals = []
    for g in range(groups):
        span = slice(g * share, (g + 1) * share)
        own = cut(tables, g * share, (g + 1) * share)
        taps = taps_all[:, :, span].reshape(3, 3 * share)
        projected = project(everything, arriving[g], inverse)
        behind = lax.ppermute(projected[-2:], "ctx", [(i, i + 1) for i in range(ctx - 1)])
        tails = jnp.where(me == 0, tails_all[:, :, span].reshape(2, 3 * share), behind)
        response, ends, last = local_filter(projected, tails, taps, own)
        states = jnp.concatenate([end_states(last), start_state[None, :, span]])
        finals.append(jnp.sum(own["final"] * states, axis=0))
        gated = gated_signal(projected, tails, taps, own, response, ends, states.reshape(-1, share))
        gated = lax.all_gather(gated, "mp", axis=0)
        total = add_outputs(gated, panel, g, order, total, f32 if g < groups - 1 else bf16)
    return (total, jnp.concatenate(finals, axis=1).T)


def solution(mesh):
    placed = (
        P("ctx", "mp"),
        P("mp"),
        P("ctx", None, "mp"),
        P(None, "mp", None),
        P(None, None, "mp"),
        P("mp", None),
        P("mp", None),
        P("mp"),
        P("mp", None),
        P("mp", "ctx"),
    )
    return jax.shard_map(
        local,
        mesh=mesh,
        in_specs=placed,
        out_specs=(P("ctx", "mp"), P("mp", None)),
        check_vma=False,
    )
```

```python
import functools
import math

import jax
import jax.numpy as jnp
from jax import lax
from jax.experimental import pallas as pl
from jax.experimental.pallas import tpu as pltpu
from jax.sharding import PartitionSpec as P

LANES = 128
SEGMENTS = 8
TAIL = 16
f32 = jnp.float32
bf16 = jnp.bfloat16


def swap_route(size, bit):
    return [(i, i ^ bit) for i in range(size)]


def tie(values, *after):
    return lax.optimization_barrier((values, after))[0]


def corner(array):
    return array[(slice(0, 1),) * (array.ndim - 2) + (slice(0, 16), slice(0, LANES))]


def near_blocks(top, bottom):
    along_x, along_y = swap_route(4, 1), swap_route(4, 2)
    return (
        lax.ppermute(top, "ctx", along_y),
        lax.ppermute(bottom, "ctx", along_x),
        lax.ppermute(top, "ctx", along_x),
        lax.ppermute(bottom, "ctx", along_y),
    )


def far_blocks(y_top, x_bottom):
    return lax.ppermute(y_top, "ctx", swap_route(4, 1)), lax.ppermute(x_bottom, "ctx", swap_route(4, 2))


def shifted_start(ref, tail_ref, back, segment):
    last = ref[pl.ds(segment - back, SEGMENTS, stride=segment), :]
    rolled = pltpu.roll(last, 1, 0)
    first = lax.broadcasted_iota(jnp.int32, rolled.shape, 0) == 0
    return jnp.where(first, jnp.broadcast_to(tail_ref[2 - back : 3 - back, :], rolled.shape), rolled)


def wide(row):
    return jnp.broadcast_to(row, (SEGMENTS, row.shape[1]))


def local_kernel(
    segment, modes, k_ref, v_ref, tail_k_ref, tail_v_ref, taps_k_ref, taps_v_ref, lam_ref, weight_ref,
    scale_ref, skip_ref, reach_ref, resp_ref, ends_ref, last_ref,
):
    lam = [wide(lam_ref[n : n + 1, :]) for n in range(modes)]
    weight = [wide(weight_ref[n : n + 1, :]) for n in range(modes)]
    tk = [wide(taps_k_ref[i : i + 1, :]) for i in range(3)]
    tv = [wide(taps_v_ref[i : i + 1, :]) for i in range(3)]
    skip = wide(skip_ref[...])
    zero = jnp.zeros((SEGMENTS, LANES), f32)

    def step(t, carry):
        k1, k2, v1, v2, state = carry
        at = pl.ds(t, SEGMENTS, stride=segment)
        k = k_ref[at, :]
        v = v_ref[at, :]
        u = (tk[0] * k + tk[1] * k1 + tk[2] * k2) * (tv[0] * v + tv[1] * v1 + tv[2] * v2)
        sums = [skip * u, zero, zero, zero]
        moved = []
        for n in range(modes):
            s = lam[n] * state[n] + u
            moved.append(s)
            sums[n % 4] = sums[n % 4] + weight[n] * s
        resp_ref[at, :] = (sums[0] + sums[1]) + (sums[2] + sums[3])
        return (k, k1, v, v1, tuple(moved))

    carry = (
        shifted_start(k_ref, tail_k_ref, 1, segment),
        shifted_start(k_ref, tail_k_ref, 2, segment),
        shifted_start(v_ref, tail_v_ref, 1, segment),
        shifted_start(v_ref, tail_v_ref, 2, segment),
        (zero,) * modes,
    )
    state = lax.fori_loop(0, segment, step, carry, unroll=4)[4]
    for n in range(modes):
        end = wide(scale_ref[n : n + 1, :]) * state[n]
        rows = slice(n * SEGMENTS, (n + 1) * SEGMENTS)
        ends_ref[rows, :] = end
        last_ref[n : n + 1, :] = jnp.sum(end * reach_ref[rows, :], axis=0, keepdims=True)


def gate_kernel(
    segment, modes, parts, q_ref, tail_q_ref, taps_q_ref, lam_ref, hop_ref, residue_ref, resp_ref, ends_ref,
    states_ref, shares_ref, gated_ref, enter_ref, wide_ref,
):
    now = shares_ref[0:modes, :] * states_ref[0:modes, :]
    for i in range(1, parts):
        rows = slice(i * modes, (i + 1) * modes)
        now = now + shares_ref[rows, :] * states_ref[rows, :]
    hop = hop_ref[...]
    for s in range(SEGMENTS):
        at = pl.ds(s, modes, stride=SEGMENTS)
        enter_ref[at, :] = now
        now = hop * now + ends_ref[at, :]
    lam = [wide(lam_ref[n : n + 1, :]) for n in range(modes)]
    taps = [wide(taps_q_ref[i : i + 1, :]) for i in range(3)]
    carried = tuple(
        wide(residue_ref[n : n + 1, :]) * lam[n] * enter_ref[n * SEGMENTS : (n + 1) * SEGMENTS, :]
        for n in range(modes)
    )

    def step(t, carry):
        q1, q2, carried = carry
        at = pl.ds(t, SEGMENTS, stride=segment)
        q = q_ref[at, :]
        sums = [resp_ref[at, :], carried[0], carried[1], carried[2]]
        for n in range(3, modes):
            sums[n % 4] = sums[n % 4] + carried[n]
        response = (sums[0] + sums[1]) + (sums[2] + sums[3])
        wide_ref[at, :] = (taps[0] * q + taps[1] * q1 + taps[2] * q2) * response
        return (q, q1, tuple(lam[n] * carried[n] for n in range(modes)))

    start = (shifted_start(q_ref, tail_q_ref, 1, segment), shifted_start(q_ref, tail_q_ref, 2, segment), carried)
    lax.fori_loop(0, segment, step, start, unroll=4)
    gated_ref[...] = wide_ref[...].astype(gated_ref.dtype)


def column(rows, first):
    return pl.BlockSpec((rows, LANES), lambda c: (0, first + c))


def local_filter(projected, tails, taps, tables):
    tokens, width = projected.shape
    blocks = width // 3 // LANES
    modes = tables["lam"].shape[0]
    flops = tokens * width // 3 * modes * 4
    return pl.pallas_call(
        functools.partial(local_kernel, tokens // SEGMENTS, modes),
        grid=(blocks,),
        in_specs=[
            column(tokens, blocks),
            column(tokens, 2 * blocks),
            column(2, blocks),
            column(2, 2 * blocks),
            column(3, blocks),
            column(3, 2 * blocks),
            column(modes, 0),
            column(modes, 0),
            column(modes, 0),
            column(1, 0),
            column(modes * SEGMENTS, 0),
        ],
        out_specs=[column(tokens, 0), column(modes * SEGMENTS, 0), column(modes, 0)],
        out_shape=[
            jax.ShapeDtypeStruct((tokens, width // 3), f32),
            jax.ShapeDtypeStruct((modes * SEGMENTS, width // 3), f32),
            jax.ShapeDtypeStruct((modes, width // 3), f32),
        ],
        cost_estimate=pl.CostEstimate(flops=flops, bytes_accessed=tokens * width * 4, transcendentals=0),
        compiler_params=pltpu.CompilerParams(vmem_limit_bytes=32 * 2**20),
        name="local_filter",
    )(
        projected, projected, tails, tails, taps, taps, tables["lam"], tables["weight"], tables["scale"],
        tables["skip"], tables["reach"],
    )


def gated_signal(projected, tails, taps, tables, response, ends, states):
    tokens, width = projected.shape
    blocks = width // 3 // LANES
    modes = tables["lam"].shape[0]
    parts = states.shape[0] // modes
    flops = tokens * width // 3 * modes * 2
    return pl.pallas_call(
        functools.partial(gate_kernel, tokens // SEGMENTS, modes, parts),
        grid=(blocks,),
        in_specs=[
            column(tokens, 0),
            column(2, 0),
            column(3, 0),
            column(modes, 0),
            column(modes, 0),
            column(modes, 0),
            column(tokens, 0),
            column(modes * SEGMENTS, 0),
            column(parts * modes, 0),
            column(parts * modes, 0),
        ],
        out_specs=column(tokens, 0),
        out_shape=jax.ShapeDtypeStruct((tokens, width // 3), bf16),
        scratch_shapes=[pltpu.VMEM((modes * SEGMENTS, LANES), f32), pltpu.VMEM((tokens, LANES), f32)],
        cost_estimate=pl.CostEstimate(flops=flops, bytes_accessed=tokens * width * 3, transcendentals=0),
        compiler_params=pltpu.CompilerParams(vmem_limit_bytes=32 * 2**20),
        name="gated_signal",
    )(
        projected, tails, taps, tables["lam"], tables["hop"], tables["residue"], response, ends, states,
        tables["shares"],
    )


def project_kernel(tails_at, offsets, slot_ref, *refs):
    count, blocks = len(offsets), len(refs) - 6 - len(offsets) - len(set(t for t, _ in tails_at))
    tail_refs = dict(zip(sorted(set(t for t, _ in tails_at)), refs[count:]))
    all_refs = refs[:count]
    block_refs = refs[count + len(tail_refs) : count + len(tail_refs) + blocks]
    inverse_ref, tail_inverse_ref, out_ref, tail_out_ref, held_ref, arrived = refs[-6:]

    def total(first_rows):
        result = None
        for n in range(count):
            rows = all_refs[n][...]
            if first_rows:
                which, at = tails_at[n]
                rows = jnp.concatenate([tail_refs[which][at : at + TAIL, :], rows], axis=0)
            weights = held_ref[slot_ref[n], offsets[n] : offsets[n] + rows.shape[1], :]
            part = jnp.dot(rows, weights, preferred_element_type=f32)
            result = part if result is None else result + part
        return result

    @pl.when(pl.program_id(0) == 0)
    def _():
        copies = [
            pltpu.make_async_copy(block_refs[n], held_ref.at[n], arrived.at[n]) for n in range(blocks)
        ]
        for copy in copies:
            copy.start()
        for copy in copies:
            copy.wait()
        result = total(True)
        tail_out_ref[...] = result[:TAIL] * tail_inverse_ref[...]
        out_ref[...] = result[TAIL:] * inverse_ref[...]

    @pl.when(pl.program_id(0) > 0)
    def _():
        out_ref[...] = total(False) * inverse_ref[...]


def project(pieces, tails_at, blocks, slots, offsets, inverse, tail_inverse):
    tokens = inverse.shape[0]
    depth, width = blocks[0].shape
    tile = math.gcd(tokens, 256)
    tail_block = tokens // (2 * TAIL)
    carriers = sorted(set(t for t, _ in tails_at))
    features = sum(piece.shape[1] for piece in pieces)
    return pl.pallas_call(
        functools.partial(project_kernel, tails_at, offsets),
        grid_spec=pltpu.PrefetchScalarGridSpec(
            num_scalar_prefetch=1,
            grid=(tokens // tile,),
            in_specs=[
                *[pl.BlockSpec((tile, piece.shape[1]), lambda m, slots: (m, 0)) for piece in pieces],
                *[pl.BlockSpec((2 * TAIL, pieces[t].shape[1]), lambda m, slots: (tail_block, 0)) for t in carriers],
                *[pl.BlockSpec(memory_space=pl.ANY) for _ in blocks],
                pl.BlockSpec((tile, 1), lambda m, slots: (m, 0)),
                pl.BlockSpec((TAIL, 1), lambda m, slots: (0, 0)),
            ],
            out_specs=[
                pl.BlockSpec((tile, width), lambda m, slots: (m, 0)),
                pl.BlockSpec((TAIL, width), lambda m, slots: (0, 0)),
            ],
            scratch_shapes=[
                pltpu.VMEM((len(blocks), depth, width), bf16),
                pltpu.SemaphoreType.DMA((len(blocks),)),
            ],
        ),
        out_shape=[jax.ShapeDtypeStruct((tokens, width), f32), jax.ShapeDtypeStruct((TAIL, width), f32)],
        cost_estimate=pl.CostEstimate(
            flops=2 * tokens * width * features, bytes_accessed=2 * features * (tokens + width), transcendentals=0
        ),
        compiler_params=pltpu.CompilerParams(vmem_limit_bytes=40 * 2**20),
        name="project",
    )(slots, *pieces, *[pieces[t] for t in carriers], *blocks, inverse, tail_inverse)


def output_kernel(count, order_ref, half_ref, *refs):
    gated_refs, panel_ref, base_refs, out_ref = refs[:count], refs[count], refs[count + 1 : -1], refs[-1]
    total = None
    for n in range(count):
        part = jnp.dot(gated_refs[n][...], panel_ref[order_ref[n]], preferred_element_type=f32)
        total = part if total is None else total + part
    for base_ref in base_refs:
        total = total + base_ref[...].astype(f32)
    out_ref[...] = total.astype(out_ref.dtype)


def add_outputs(gated, order, panel, group, half, bases, dtype):
    tokens, share = gated[0].shape
    chips, columns = panel.shape[0], panel.shape[2] // 2
    tile = math.gcd(tokens, 256)
    return pl.pallas_call(
        functools.partial(output_kernel, len(gated)),
        grid_spec=pltpu.PrefetchScalarGridSpec(
            num_scalar_prefetch=2,
            grid=(tokens // tile,),
            in_specs=[
                *[pl.BlockSpec((tile, share), lambda m, order, half: (m, 0)) for _ in gated],
                pl.BlockSpec((chips, share, columns), lambda m, order, half: (0, group, half[0])),
                *[pl.BlockSpec((tile, columns), lambda m, order, half: (m, 0)) for _ in bases],
            ],
            out_specs=pl.BlockSpec((tile, columns), lambda m, order, half: (m, 0)),
        ),
        out_shape=jax.ShapeDtypeStruct((tokens, columns), dtype),
        cost_estimate=pl.CostEstimate(
            flops=2 * tokens * columns * len(gated) * share, bytes_accessed=4 * tokens * columns, transcendentals=0
        ),
        compiler_params=pltpu.CompilerParams(vmem_limit_bytes=40 * 2**20),
        name="add_outputs",
    )(order, half, *gated, panel, *bases)


def exchange(rows, axis, masks):
    size = lax.axis_size(axis)
    return [
        rows[n] if mask == 0 else lax.ppermute(rows[n], axis, swap_route(size, mask)) for n, mask in enumerate(masks)
    ]


def ring(block, rounds):
    size = lax.axis_size("mp")
    blocks = [block]
    for _ in range(rounds):
        blocks.append(lax.ppermute(blocks[-1], "mp", [(i, (i + 2) % size) for i in range(size)]))
    return blocks


def core_swap(block):
    return lax.ppermute(block, "mp", swap_route(lax.axis_size("mp"), 1))


def ctx_order():
    size = lax.axis_size("ctx")
    index = jnp.arange(size)
    return lax.axis_index("ctx") ^ index if (size, lax.axis_size("mp")) == (4, 8) else index


def filter_tables(decay_rate, residue, skip_gain, tokens):
    me = lax.axis_index("ctx")
    size = lax.axis_size("ctx")
    rate = decay_rate.T
    modes, channels = rate.shape
    scale = jnp.sqrt(-jnp.expm1(-2.0 * rate))
    segment = tokens // SEGMENTS
    ahead = (SEGMENTS - 1 - jnp.arange(SEGMENTS, dtype=f32)) * segment
    reach = jnp.exp(-rate[:, None, :] * ahead[None, :, None]).reshape(modes * SEGMENTS, channels)
    index = ctx_order()
    gap = (me - 1 - index).astype(f32) * tokens
    shares = jnp.where(
        (index < me)[:, None, None], jnp.exp(-rate[None] * jnp.maximum(gap, 0.0)[:, None, None]), 0.0
    )
    first = jnp.exp(-rate * (me * tokens).astype(f32))[None]
    final_gap = (size - 1 - index).astype(f32) * tokens
    final = jnp.exp(-rate[None] * final_gap[:, None, None])
    final_first = jnp.exp(-rate * (size * tokens))[None]
    return {
        "lam": jnp.exp(-rate),
        "hop": jnp.exp(-rate * segment),
        "weight": residue.T * scale,
        "residue": residue.T,
        "scale": scale,
        "skip": skip_gain[None, :],
        "reach": reach,
        "shares": jnp.concatenate([shares, first]).reshape((size + 1) * modes, channels),
        "final": jnp.concatenate([final, final_first]),
    }


def cut(tables, start, stop):
    return {name: table[..., start:stop] for name, table in tables.items()}


def local(
    activations,
    norm_gain,
    w_in,
    tail_rows,
    short_filter,
    decay_rate,
    residue,
    skip_gain,
    state_in,
    w_out,
):
    tokens, features = activations.shape
    channels = w_in.shape[2]
    mp = lax.axis_size("mp")
    ctx = lax.axis_size("ctx")
    me = lax.axis_index("ctx")
    model_width = features * mp
    groups = 2 if channels % (2 * LANES) == 0 else 1
    share = channels // groups
    half = w_in.shape[0] // 2
    here = lax.axis_index("mp")
    chips = mp // 2
    chip, core = here // 2, here % 2
    special = (ctx, mp) == (4, 8)

    behind = lax.ppermute(activations[-TAIL:], "ctx", [(i, i + 1) for i in range(ctx - 1)])
    w_parts = [
        [w_in[top : top + half, :, g * share : (g + 1) * share].reshape(half, 3 * share) for top in (0, half)]
        for g in range(groups)
    ]
    act_float = activations.astype(f32)
    tail_float = behind.astype(f32)
    scaled = (act_float * norm_gain[None, :]).astype(bf16)
    scaled_tail = (tail_float * norm_gain[None, :]).astype(bf16)
    squares = jnp.concatenate([jnp.sum(tail_float * tail_float, axis=1), jnp.sum(act_float * act_float, axis=1)])
    tables = filter_tables(decay_rate, residue, skip_gain, tokens)
    start_state = state_in.T
    tails_in = tail_rows.transpose(2, 0, 1).astype(f32)

    if special:
        part = features // 2
        first = scaled[:, :part]
        second = jnp.concatenate([scaled[:, part:], scaled_tail[:, :part], scaled_tail[:, part:]])
        near = [near_blocks(*w_parts[0])]
        first, second = ring(first, chips - 1), ring(second, chips - 1)
        other_first, other_second = [core_swap(p) for p in first], [core_swap(p) for p in second]
        pieces = first + second + other_first + other_second
        tails_at = [(n % 4 + 4 + 8 * (n // 8), TAIL * (n // 4 % 2)) for n in range(16)]
        offsets = [part * (n // 4 % 2) for n in range(16)]
        slots = jnp.stack([2 * (me ^ ((chip - n % 4) % chips)) + (core ^ (n // 8)) for n in range(16)])
        squares = squares[None] + core_swap(squares[None])
        squares = sum(exchange([squares] * chips, "mp", range(0, mp, 2)))[0]
        mine = w_out.reshape(ctx, channels // ctx, -1)
        mine = tie(mine, corner(near[0][0]), corner(near[0][1]))
        sent = [lax.dynamic_index_in_dim(mine, me ^ d, 0, False) for d in range(ctx)]
        by_owner = jnp.stack(exchange(sent, "ctx", range(ctx)))
        by_owner = tie(by_owner, corner(second[2]))
        sent = [lax.dynamic_index_in_dim(by_owner, (chip ^ d) ^ me, 0, False) for d in range(chips)]
        my_rows = jnp.stack(exchange(sent, "mp", range(0, mp, 2)))
    else:
        extended = jnp.concatenate([scaled, scaled_tail, scaled_tail])
        everything = lax.all_gather(extended, "mp", axis=0)
        pieces = [everything[n] for n in range(mp)]
        tails_at = [(n, 0) for n in range(mp)]
        offsets = [n * features % half for n in range(mp)]
        slots = jnp.asarray([n * features // half for n in range(mp)])
        squares = lax.psum(squares, "mp")
        groups_of_core = [[i for i in range(mp) if i % 2 == c] for c in range(2)]
        rows = lax.all_to_all(w_out.reshape(ctx, channels // ctx, -1), "ctx", 0, 0)
        rows = rows.reshape(ctx, channels // ctx, chips // ctx, -1).swapaxes(1, 2)
        rows = rows.reshape(chips, channels // ctx, -1)
        rows = lax.all_to_all(rows, "mp", 0, 0, axis_index_groups=groups_of_core)
        panel = lax.all_gather(rows, "ctx", axis=1).reshape(chips, channels, -1)

    inverse = lax.rsqrt(squares / model_width + 1e-06)[:, None]
    inverse, tail_inverse = inverse[TAIL:], inverse[:TAIL]
    slots = slots.astype(jnp.int32)
    finals = []
    rings = []
    after_states = None
    for g in range(groups):
        span = slice(g * share, (g + 1) * share)
        own = cut(tables, g * share, (g + 1) * share)
        taps = short_filter[:, :, span].reshape(3, 3 * share)
        if special:
            if g > 0:
                near.append(near_blocks(*tie(w_parts[g], corner(near[g - 1][2]), corner(near[g - 1][3]))))
            y_top, x_bottom, x_top, y_bottom = near[g]
            far_top, far_bottom = far_blocks(*(tie((y_top, x_bottom), after_states) if g > 0 else (y_top, x_bottom)))
            blocks = [*w_parts[g], x_top, x_bottom, y_top, y_bottom, far_top, far_bottom]
        else:
            gathered = [lax.all_gather(p, "ctx", axis=0) for p in w_parts[g]]
            blocks = [gathered[n % 2][n // 2] for n in range(2 * ctx)]
        projected, before = project(pieces, tails_at, blocks, slots, offsets, inverse, tail_inverse)
        tails = jnp.where(me == 0, tails_in[:, :, span].reshape(2, 3 * share), before[TAIL - 2 :])
        response, ends, last = local_filter(projected, tails, taps, own)
        if special:
            lasts = jnp.stack(exchange([last] * ctx, "ctx", range(ctx)))
            after_states = lasts[:, :8, :LANES]
        else:
            lasts = lax.all_gather(last, "ctx", axis=0)
        states = jnp.concatenate([lasts, start_state[None, :, span]])
        finals.append(jnp.sum(own["final"] * states, axis=0))
        gated = gated_signal(projected, tails, taps, own, response, ends, states.reshape(-1, share))
        if special:
            rings.append(ring(gated, chips - 1))
        else:
            gathered = lax.all_gather(gated, "mp", axis=0, axis_index_groups=groups_of_core)
            rings.append([gathered[n] for n in range(chips)])

    if special:
        top, bottom = tie((my_rows[: chips // 2], my_rows[chips // 2 :]), after_states)
        y_top, x_bottom, x_top, y_bottom = near_blocks(top, bottom)
        far_top, far_bottom = far_blocks(y_top, x_bottom)
        panel = jnp.zeros((chips, ctx, *my_rows.shape[1:]), bf16)
        arrived = [
            (0, top, bottom), (1, x_top, x_bottom), (2, y_top, y_bottom), (3, far_top, far_bottom),
        ]
        for d, upper, lower in arrived:
            panel = lax.dynamic_update_slice(panel, upper[:, None], (0, me ^ d, 0, 0))
            panel = lax.dynamic_update_slice(panel, lower[:, None], (chips // 2, me ^ d, 0, 0))
        panel = panel.reshape(chips, channels, -1)
        order = jnp.stack([((chip - n) % chips) ^ chip for n in range(chips)])
    else:
        order = jnp.arange(chips)
    order = order.astype(jnp.int32)
    mine, other = core[None].astype(jnp.int32), (1 - core)[None].astype(jnp.int32)
    kept, given = [activations], []
    for g in range(groups):
        final = g == groups - 1
        steps = [slice(0, chips - 1), slice(chips - 1, chips)] if final else [slice(0, chips)]
        for n, step in enumerate(steps):
            dtype = bf16 if final and n == len(steps) - 1 else f32
            given = [add_outputs(rings[g][step], order[step], panel, g, other, given, dtype)]
            kept = [add_outputs(rings[g][step], order[step], panel, g, mine, kept, f32)]
    total = (kept[0] + core_swap(given[0]).astype(f32)).astype(bf16)
    return (total, jnp.concatenate(finals, axis=1).T)


def solution(mesh):
    placed = (
        P("ctx", "mp"),
        P("mp"),
        P("ctx", None, "mp"),
        P(None, "mp", None),
        P(None, None, "mp"),
        P("mp", None),
        P("mp", None),
        P("mp"),
        P("mp", None),
        P("mp", "ctx"),
    )
    return jax.shard_map(
        local,
        mesh=mesh,
        in_specs=placed,
        out_specs=(P("ctx", "mp"), P("mp", None)),
        check_vma=False,
    )
```

```python
import functools
import math

import jax
import jax.numpy as jnp
from jax import lax
from jax.experimental import pallas as pl
from jax.experimental.pallas import tpu as pltpu
from jax.sharding import PartitionSpec as P

LANES = 128
SEGMENTS = 8
TAIL = 16
f32 = jnp.float32
bf16 = jnp.bfloat16


def swap_route(size, bit):
    return [(i, i ^ bit) for i in range(size)]


def send(transfers, after=()):
    arrays = {id(array): array for array, _, _ in transfers}
    if len(after) > 0:
        tied = lax.optimization_barrier((list(arrays.values()), tuple(after)))[0]
        arrays = dict(zip(arrays, tied))
    return [lax.ppermute(arrays[id(array)], axis, route) for array, axis, route in transfers]


def shifted_start(ref, tail_ref, back, segment):
    last = ref[pl.ds(segment - back, SEGMENTS, stride=segment), :]
    rolled = pltpu.roll(last, 1, 0)
    first = lax.broadcasted_iota(jnp.int32, rolled.shape, 0) == 0
    return jnp.where(first, jnp.broadcast_to(tail_ref[2 - back : 3 - back, :], rolled.shape), rolled)


def wide(row):
    return jnp.broadcast_to(row, (SEGMENTS, row.shape[1]))


def local_kernel(
    segment, modes, k_ref, v_ref, tail_k_ref, tail_v_ref, taps_k_ref, taps_v_ref, lam_ref, weight_ref,
    scale_ref, skip_ref, reach_ref, resp_ref, ends_ref, last_ref,
):
    lam = [wide(lam_ref[n : n + 1, :]) for n in range(modes)]
    weight = [wide(weight_ref[n : n + 1, :]) for n in range(modes)]
    tk = [wide(taps_k_ref[i : i + 1, :]) for i in range(3)]
    tv = [wide(taps_v_ref[i : i + 1, :]) for i in range(3)]
    skip = wide(skip_ref[...])
    zero = jnp.zeros((SEGMENTS, LANES), f32)

    def step(t, carry):
        k1, k2, v1, v2, state = carry
        at = pl.ds(t, SEGMENTS, stride=segment)
        k = k_ref[at, :]
        v = v_ref[at, :]
        u = (tk[0] * k + tk[1] * k1 + tk[2] * k2) * (tv[0] * v + tv[1] * v1 + tv[2] * v2)
        sums = [skip * u, zero, zero, zero]
        moved = []
        for n in range(modes):
            s = lam[n] * state[n] + u
            moved.append(s)
            sums[n % 4] = sums[n % 4] + weight[n] * s
        resp_ref[at, :] = (sums[0] + sums[1]) + (sums[2] + sums[3])
        return (k, k1, v, v1, tuple(moved))

    carry = (
        shifted_start(k_ref, tail_k_ref, 1, segment),
        shifted_start(k_ref, tail_k_ref, 2, segment),
        shifted_start(v_ref, tail_v_ref, 1, segment),
        shifted_start(v_ref, tail_v_ref, 2, segment),
        (zero,) * modes,
    )
    state = lax.fori_loop(0, segment, step, carry, unroll=4)[4]
    for n in range(modes):
        end = wide(scale_ref[n : n + 1, :]) * state[n]
        rows = slice(n * SEGMENTS, (n + 1) * SEGMENTS)
        ends_ref[rows, :] = end
        last_ref[n : n + 1, :] = jnp.sum(end * reach_ref[rows, :], axis=0, keepdims=True)


def gate_kernel(
    segment, modes, parts, q_ref, tail_q_ref, taps_q_ref, lam_ref, hop_ref, residue_ref, resp_ref, ends_ref,
    states_ref, shares_ref, gated_ref, enter_ref, wide_ref,
):
    now = shares_ref[0:modes, :] * states_ref[0:modes, :]
    for i in range(1, parts):
        rows = slice(i * modes, (i + 1) * modes)
        now = now + shares_ref[rows, :] * states_ref[rows, :]
    hop = hop_ref[...]
    for s in range(SEGMENTS):
        at = pl.ds(s, modes, stride=SEGMENTS)
        enter_ref[at, :] = now
        now = hop * now + ends_ref[at, :]
    lam = [wide(lam_ref[n : n + 1, :]) for n in range(modes)]
    taps = [wide(taps_q_ref[i : i + 1, :]) for i in range(3)]
    carried = tuple(
        wide(residue_ref[n : n + 1, :]) * lam[n] * enter_ref[n * SEGMENTS : (n + 1) * SEGMENTS, :]
        for n in range(modes)
    )

    def step(t, carry):
        q1, q2, carried = carry
        at = pl.ds(t, SEGMENTS, stride=segment)
        q = q_ref[at, :]
        sums = [resp_ref[at, :], carried[0], carried[1], carried[2]]
        for n in range(3, modes):
            sums[n % 4] = sums[n % 4] + carried[n]
        response = (sums[0] + sums[1]) + (sums[2] + sums[3])
        wide_ref[at, :] = (taps[0] * q + taps[1] * q1 + taps[2] * q2) * response
        return (q, q1, tuple(lam[n] * carried[n] for n in range(modes)))

    start = (shifted_start(q_ref, tail_q_ref, 1, segment), shifted_start(q_ref, tail_q_ref, 2, segment), carried)
    lax.fori_loop(0, segment, step, start, unroll=4)
    gated_ref[...] = wide_ref[...].astype(gated_ref.dtype)


def column(rows, first):
    return pl.BlockSpec((rows, LANES), lambda c: (0, first + c))


def local_filter(projected, tails, taps, tables):
    tokens, width = projected.shape
    blocks = width // 3 // LANES
    modes = tables["lam"].shape[0]
    flops = 0
    return pl.pallas_call(
        functools.partial(local_kernel, tokens // SEGMENTS, modes),
        grid=(blocks,),
        in_specs=[
            column(tokens, blocks),
            column(tokens, 2 * blocks),
            column(2, blocks),
            column(2, 2 * blocks),
            column(3, blocks),
            column(3, 2 * blocks),
            column(modes, 0),
            column(modes, 0),
            column(modes, 0),
            column(1, 0),
            column(modes * SEGMENTS, 0),
        ],
        out_specs=[column(tokens, 0), column(modes * SEGMENTS, 0), column(modes, 0)],
        out_shape=[
            jax.ShapeDtypeStruct((tokens, width // 3), f32),
            jax.ShapeDtypeStruct((modes * SEGMENTS, width // 3), f32),
            jax.ShapeDtypeStruct((modes, width // 3), f32),
        ],
        cost_estimate=pl.CostEstimate(flops=flops, bytes_accessed=tokens * width * 4, transcendentals=0),
        compiler_params=pltpu.CompilerParams(vmem_limit_bytes=32 * 2**20),
        name="local_filter",
    )(
        projected, projected, tails, tails, taps, taps, tables["lam"], tables["weight"], tables["scale"],
        tables["skip"], tables["reach"],
    )


def gated_signal(projected, tails, taps, tables, response, ends, states, lane):
    tokens, width = projected.shape
    modes = tables["lam"].shape[0]
    parts = states.shape[0] // modes
    flops = 0
    return pl.pallas_call(
        functools.partial(gate_kernel, tokens // SEGMENTS, modes, parts),
        grid=(1,),
        in_specs=[
            column(tokens, lane),
            column(2, lane),
            column(3, lane),
            column(modes, lane),
            column(modes, lane),
            column(modes, lane),
            column(tokens, lane),
            column(modes * SEGMENTS, lane),
            column(parts * modes, lane),
            column(parts * modes, lane),
        ],
        out_specs=column(tokens, 0),
        out_shape=jax.ShapeDtypeStruct((tokens, LANES), bf16),
        scratch_shapes=[pltpu.VMEM((modes * SEGMENTS, LANES), f32), pltpu.VMEM((tokens, LANES), f32)],
        cost_estimate=pl.CostEstimate(flops=flops, bytes_accessed=tokens * width * 3, transcendentals=0),
        compiler_params=pltpu.CompilerParams(vmem_limit_bytes=32 * 2**20),
        name="gated_signal",
    )(
        projected, tails, taps, tables["lam"], tables["hop"], tables["residue"], response, ends, states,
        tables["shares"],
    )


def project_kernel(order_ref, all_ref, tails_ref, *refs):
    unit_refs, (inverse_ref, tail_inverse_ref, out_ref, tail_out_ref) = refs[:-4], refs[-4:]
    features = all_ref.shape[2]
    chunks = [(ref, at) for ref in unit_refs for at in range(0, ref.shape[0], features)]

    def total(first_rows):
        result = None
        for n, (ref, at) in enumerate(chunks):
            block = all_ref[order_ref[n]]
            if first_rows:
                block = jnp.concatenate([tails_ref[order_ref[len(chunks) + n]], block], axis=0)
            part = jnp.dot(block, ref[at : at + features, :], preferred_element_type=f32)
            result = part if result is None else result + part
        return result

    @pl.when(pl.program_id(0) == 0)
    def _():
        result = total(True)
        tail_out_ref[...] = result[:TAIL] * tail_inverse_ref[...]
        out_ref[...] = result[TAIL:] * inverse_ref[...]

    @pl.when(pl.program_id(0) > 0)
    def _():
        out_ref[...] = total(False) * inverse_ref[...]


def project(everything, tails, units, order, inverse, tail_inverse):
    mp, tokens, features = everything.shape
    width = units[0].shape[1]
    tile = math.gcd(tokens, 256)
    return pl.pallas_call(
        project_kernel,
        grid_spec=pltpu.PrefetchScalarGridSpec(
            num_scalar_prefetch=1,
            grid=(tokens // tile,),
            in_specs=[
                pl.BlockSpec((mp, tile, features), lambda m, order: (0, m, 0)),
                pl.BlockSpec((mp, TAIL, features), lambda m, order: (0, 0, 0)),
                *[pl.BlockSpec(memory_space=pltpu.VMEM) for _ in units],
                pl.BlockSpec((tile, 1), lambda m, order: (m, 0)),
                pl.BlockSpec((TAIL, 1), lambda m, order: (0, 0)),
            ],
            out_specs=[
                pl.BlockSpec((tile, width), lambda m, order: (m, 0)),
                pl.BlockSpec((TAIL, width), lambda m, order: (0, 0)),
            ],
        ),
        out_shape=[jax.ShapeDtypeStruct((tokens, width), f32), jax.ShapeDtypeStruct((TAIL, width), f32)],
        compiler_params=pltpu.CompilerParams(vmem_limit_bytes=40 * 2**20),
        name="project",
    )(order, everything, tails, *units, inverse, tail_inverse)


def output_kernel(chips, order_ref, half_ref, *refs):
    count = len(chips[0])
    gated_refs = refs[: count * len(chips)]
    panel_ref, base_refs, out_ref = refs[len(gated_refs)], refs[len(gated_refs) + 1 : -1], refs[-1]
    total = None
    for n, chip in enumerate(chips):
        rows = [ref[...] for ref in gated_refs[n * count : (n + 1) * count]]
        rows = jnp.concatenate(rows, axis=1) if count > 1 else rows[0]
        part = jnp.dot(rows, panel_ref[order_ref[n]], preferred_element_type=f32)
        total = part if total is None else total + part
    for base_ref in base_refs:
        total = total + base_ref[...].astype(f32)
    out_ref[...] = total.astype(out_ref.dtype)


def add_outputs(gated, order, panel, group, half, bases, dtype):
    tokens = gated[0][0].shape[0]
    share = len(gated[0]) * LANES
    chips, columns = panel.shape[0], panel.shape[2] // 2
    tile = math.gcd(tokens, 256)
    blocks = [block for chip in gated for block in chip]
    return pl.pallas_call(
        functools.partial(output_kernel, [[0] * len(chip) for chip in gated]),
        grid_spec=pltpu.PrefetchScalarGridSpec(
            num_scalar_prefetch=2,
            grid=(tokens // tile,),
            in_specs=[
                *[pl.BlockSpec((tile, LANES), lambda m, order, half: (m, 0)) for _ in blocks],
                pl.BlockSpec((chips, share, columns), lambda m, order, half: (0, group, half[0])),
                *[pl.BlockSpec((tile, columns), lambda m, order, half: (m, 0)) for _ in bases],
            ],
            out_specs=pl.BlockSpec((tile, columns), lambda m, order, half: (m, 0)),
        ),
        out_shape=jax.ShapeDtypeStruct((tokens, columns), dtype),
        cost_estimate=pl.CostEstimate(
            flops=4 * tokens * columns * len(gated) * share, bytes_accessed=4 * tokens * columns, transcendentals=0
        ),
        compiler_params=pltpu.CompilerParams(vmem_limit_bytes=32 * 2**20),
        name="add_outputs",
    )(order, half, *blocks, panel, *bases)


def core_swap(block):
    return lax.ppermute(block, "mp", swap_route(lax.axis_size("mp"), 1))


def ctx_order():
    size = lax.axis_size("ctx")
    index = jnp.arange(size)
    return lax.axis_index("ctx") ^ index if (size, lax.axis_size("mp")) == (4, 8) else index


def filter_tables(decay_rate, residue, skip_gain, tokens):
    me = lax.axis_index("ctx")
    size = lax.axis_size("ctx")
    rate = decay_rate.T
    modes, channels = rate.shape
    scale = jnp.sqrt(-jnp.expm1(-2.0 * rate))
    segment = tokens // SEGMENTS
    ahead = (SEGMENTS - 1 - jnp.arange(SEGMENTS, dtype=f32)) * segment
    reach = jnp.exp(-rate[:, None, :] * ahead[None, :, None]).reshape(modes * SEGMENTS, channels)
    index = ctx_order()
    gap = (me - 1 - index).astype(f32) * tokens
    shares = jnp.where(
        (index < me)[:, None, None], jnp.exp(-rate[None] * jnp.maximum(gap, 0.0)[:, None, None]), 0.0
    )
    first = jnp.exp(-rate * (me * tokens).astype(f32))[None]
    final_gap = (size - 1 - index).astype(f32) * tokens
    final = jnp.exp(-rate[None] * final_gap[:, None, None])
    final_first = jnp.exp(-rate * (size * tokens))[None]
    return {
        "lam": jnp.exp(-rate),
        "hop": jnp.exp(-rate * segment),
        "weight": residue.T * scale,
        "residue": residue.T,
        "scale": scale,
        "skip": skip_gain[None, :],
        "reach": reach,
        "shares": jnp.concatenate([shares, first]).reshape((size + 1) * modes, channels),
        "final": jnp.concatenate([final, final_first]),
    }


def cut(tables, start, stop):
    return {name: table[..., start:stop] for name, table in tables.items()}


def local(
    activations,
    norm_gain,
    w_in,
    tail_rows,
    short_filter,
    decay_rate,
    residue,
    skip_gain,
    state_in,
    w_out,
):
    tokens, features = activations.shape
    channels = w_in.shape[2]
    mp = lax.axis_size("mp")
    ctx = lax.axis_size("ctx")
    me = lax.axis_index("ctx")
    model_width = features * mp
    groups = 2 if channels % (2 * LANES) == 0 else 1
    share = channels // groups
    here = lax.axis_index("mp")
    chips = mp // 2
    chip, core = here // 2, here % 2
    special = (ctx, mp, groups) == (4, 8, 2)
    per = mp // ctx

    act_float = activations.astype(f32)
    scaled = (act_float * norm_gain[None, :]).astype(bf16)
    everything = lax.all_gather(scaled, "mp", axis=0)
    w_units = [w_in[:, :, g * share : (g + 1) * share].reshape(-1, 3 * share) for g in range(groups)]
    next_on = ("ctx", [(i, i + 1) for i in range(ctx - 1)])
    tails_all = lax.ppermute(scaled[-TAIL:], *next_on)[None]
    squares = jnp.sum(act_float * act_float, axis=1)[None]
    tables = filter_tables(decay_rate, residue, skip_gain, tokens)
    start_state = state_in.T
    tails_in = tail_rows.transpose(2, 0, 1).astype(f32)
    columns = w_out.shape[1] // per

    if special:
        along_x, along_y, across = (("ctx", swap_route(ctx, mask)) for mask in (1, 2, 3))
        along_z = ("mp", [(i, (i + 2) % mp) for i in range(mp)])
        others = [("mp", swap_route(mp, 2 * d)) for d in range(1, chips)]
        middle, quarter = w_in.shape[0] // 2, w_in.shape[0] // 4
        own_rows = w_out.reshape(ctx, channels // ctx, -1)
        sent = [lax.dynamic_index_in_dim(own_rows, me ^ d, 0, False) for d in range(ctx)]
        near = send([(w_units[0], *along_x), (w_units[0], *along_y)])
        squares = squares + core_swap(squares)
        squares = squares + sum(lax.ppermute(squares, *route) for route in others)
        inverse = lax.rsqrt(squares[0] / model_width + 1e-06)[:, None]
        tail_inverse = lax.ppermute(inverse[-TAIL:], *next_on)
        first_near = near
        near, sent = lax.optimization_barrier(((near, sent), inverse))[0]
        far = send([(near[1][:middle], *along_x), (near[0][middle:], *along_y)])
        units = [[w_units[0], *near, *far]]
        got = send([(sent[1], *along_x), (sent[2], *along_y), (sent[3], *across)], first_near)
        by_owner = jnp.stack([sent[0], *got])
        tails_all = jnp.concatenate([tails_all, core_swap(tails_all)])
        tails_all = jnp.concatenate([tails_all, *[lax.ppermute(tails_all, *route) for route in others]])
        near = send([(w_units[1], *along_x), (w_units[1], *along_y)], [*far, *got, tails_all, tail_inverse])
        order = jnp.stack([(me ^ (n // per)) * per + n % per for n in range(mp)]).astype(jnp.int32)
        order = jnp.concatenate([order, order ^ here])

        sent = [lax.dynamic_index_in_dim(by_owner, (chip ^ d) ^ me, 0, False) for d in range(chips)]
        own_row, *sent = lax.optimization_barrier((sent, everything))[0]
        by_chip = [lax.ppermute(block, *route) for block, route in zip(sent, others)]
        rows = jnp.stack([own_row, *by_chip])
        panel_order = jnp.stack([((chip - n) % chips) ^ chip for n in range(chips)]).astype(jnp.int32)
    else:
        units = []
        for g in range(groups):
            gathered = lax.all_gather(w_units[g], "ctx", axis=0)
            units.append([gathered[n] for n in range(ctx)])
        order = jnp.tile(jnp.arange(mp, dtype=jnp.int32), 2)
        tails_all = lax.all_gather(tails_all[0], "mp", axis=0)
        inverse = lax.rsqrt(lax.psum(squares, "mp")[0] / model_width + 1e-06)[:, None]
        tail_inverse = lax.ppermute(inverse[-TAIL:], *next_on)
        groups_of_core = [[i for i in range(mp) if i % 2 == c] for c in range(2)]
        rows = lax.all_to_all(w_out.reshape(ctx, channels // ctx, -1), "ctx", 0, 0)
        rows = rows.reshape(ctx, channels // ctx, chips // ctx, 2 * columns).swapaxes(1, 2)
        rows = rows.reshape(chips, channels // ctx, 2 * columns)
        rows = lax.all_to_all(rows, "mp", 0, 0, axis_index_groups=groups_of_core)
        panel = lax.all_gather(rows, "ctx", axis=1).reshape(chips, channels, 2 * columns)
        panel_order = jnp.arange(chips, dtype=jnp.int32)

    finals = []
    rings = []
    for g in range(groups):
        span = slice(g * share, (g + 1) * share)
        own = cut(tables, g * share, (g + 1) * share)
        taps = short_filter[:, :, span].reshape(3, 3 * share)
        if rings:
            order = lax.optimization_barrier((order, gated))[0]
        projected, before = project(everything, tails_all, units[g], order, inverse, tail_inverse)
        tails = jnp.where(me == 0, tails_in[:, :, span].reshape(2, 3 * share), before[TAIL - 2 :])
        if special and g > 0:
            tails = lax.optimization_barrier((tails, rings[0][1]))[0]
        response, ends, last = local_filter(projected, tails, taps, own)
        if special:
            shared = lax.optimization_barrier((last, by_chip[0]))[0] if g == 0 else last
            arrived = [lax.ppermute(shared, *route) for route in (along_x, along_y, across)]
            if g == 0:
                near = lax.optimization_barrier((near, before))[0]
                far = send([(near[1][:quarter], *along_x), (near[0][middle : middle + quarter], *along_y)])
                arrived = lax.optimization_barrier((arrived, (*by_chip, *far)))[0]
                late = send([(near[1][quarter:middle], *along_x), (near[0][middle + quarter :], *along_y)], arrived)
            else:
                arrived = lax.optimization_barrier((arrived, rings[0][2]))[0]
                panel_bottom = send([(bottom, *along_x), (bottom, *along_y)], arrived)
                panel_far = send([(panel_top[1], *along_x), (panel_bottom[0], *along_y)])
            lasts = jnp.stack([last, *arrived])
        else:
            lasts = lax.all_gather(last, "ctx", axis=0)
        states = jnp.concatenate([lasts, start_state[None, :, span]])
        finals.append(jnp.sum(own["final"] * states, axis=0))
        gated = [
            gated_signal(projected, tails, taps, own, response, ends, states.reshape(-1, share), lane)
            for lane in range(share // LANES)
        ]
        if special:
            blocks = [gated]
            for _ in range(chips - 1):
                blocks.append([lax.ppermute(block, *along_z) for block in blocks[-1]])
            rings.append(blocks)
            if g == 0:
                units.append([w_units[1], *near, *[jnp.concatenate(pair) for pair in zip(far, late)]])
                top, bottom = rows[: chips // 2], rows[chips // 2 :]
                panel_top = send([(top, *along_x), (top, *along_y)], [*late, *gated])
        else:
            gathered = [lax.all_gather(block, "mp", axis=0, axis_index_groups=groups_of_core) for block in gated]
            rings.append([[block[n] for block in gathered] for n in range(chips)])

    if special:
        panel = jnp.zeros((chips, ctx, *rows.shape[1:]), bf16)
        landed = [(0, 0, rows), (3, 0, panel_far[0]), (3, 2, panel_far[1])]
        landed += [(1 + n, 0, panel_top[n]) for n in range(2)] + [(1 + n, 2, panel_bottom[n]) for n in range(2)]
        for d, first, block in landed:
            panel = lax.dynamic_update_slice(panel, block[:, None], (first, me ^ d, 0, 0))
        panel = panel.reshape(chips, channels, 2 * columns)
    mine, other = core[None].astype(jnp.int32), (1 - core)[None].astype(jnp.int32)
    kept, given = [activations], []
    for g in range(groups):
        final = g == groups - 1
        steps = [slice(0, chips - 1), slice(chips - 1, chips)] if final else [slice(0, chips)]
        for n, step in enumerate(steps):
            dtype = bf16 if final and n == len(steps) - 1 else f32
            last_step = rings[g][step]
            if final and n == len(steps) - 1:
                last_step = lax.optimization_barrier((last_step, kept[0]))[0]
            given = [add_outputs(last_step, panel_order[step], panel, g, other, given, dtype)]
            kept = [add_outputs(last_step, panel_order[step], panel, g, mine, kept, f32)]
    total = (kept[0] + core_swap(given[0]).astype(f32)).astype(bf16)
    return (total, jnp.concatenate(finals, axis=1).T)


def solution(mesh):
    placed = (
        P("ctx", "mp"),
        P("mp"),
        P("ctx", None, "mp"),
        P(None, "mp", None),
        P(None, None, "mp"),
        P("mp", None),
        P("mp", None),
        P("mp"),
        P("mp", None),
        P("mp", "ctx"),
    )
    return jax.shard_map(
        local,
        mesh=mesh,
        in_specs=placed,
        out_specs=(P("ctx", "mp"), P("mp", None)),
        check_vma=False,
    )
```

```python
import functools
import math

import jax
import jax.numpy as jnp
from jax import lax
from jax.experimental import pallas as pl
from jax.experimental.pallas import tpu as pltpu
from jax.sharding import PartitionSpec as P

LANES = 128
SEGMENTS = 8
TAIL = 16
f32 = jnp.float32
bf16 = jnp.bfloat16


def swap_route(size, bit):
    return [(i, i ^ bit) for i in range(size)]


def send(transfers, after=()):
    arrays = {id(array): array for array, _, _ in transfers}
    if len(after) > 0:
        tied = lax.optimization_barrier((list(arrays.values()), tuple(after)))[0]
        arrays = dict(zip(arrays, tied))
    return [lax.ppermute(arrays[id(array)], axis, route) for array, axis, route in transfers]


def shifted_start(ref, tail_ref, back, segment):
    last = ref[pl.ds(segment - back, SEGMENTS, stride=segment), :]
    rolled = pltpu.roll(last, 1, 0)
    first = lax.broadcasted_iota(jnp.int32, rolled.shape, 0) == 0
    return jnp.where(first, jnp.broadcast_to(tail_ref[2 - back : 3 - back, :], rolled.shape), rolled)


def wide(row):
    return jnp.broadcast_to(row, (SEGMENTS, row.shape[1]))


def local_kernel(
    segment, modes, k_ref, v_ref, tail_k_ref, tail_v_ref, taps_k_ref, taps_v_ref, lam_ref, weight_ref,
    scale_ref, skip_ref, reach_ref, resp_ref, ends_ref, last_ref,
):
    lam = [wide(lam_ref[n : n + 1, :]) for n in range(modes)]
    weight = [wide(weight_ref[n : n + 1, :]) for n in range(modes)]
    tk = [wide(taps_k_ref[i : i + 1, :]) for i in range(3)]
    tv = [wide(taps_v_ref[i : i + 1, :]) for i in range(3)]
    skip = wide(skip_ref[...])
    zero = jnp.zeros((SEGMENTS, LANES), f32)

    def step(t, carry):
        k1, k2, v1, v2, state = carry
        at = pl.ds(t, SEGMENTS, stride=segment)
        k = k_ref[at, :]
        v = v_ref[at, :]
        u = (tk[0] * k + tk[1] * k1 + tk[2] * k2) * (tv[0] * v + tv[1] * v1 + tv[2] * v2)
        sums = [skip * u, zero, zero, zero]
        moved = []
        for n in range(modes):
            s = lam[n] * state[n] + u
            moved.append(s)
            sums[n % 4] = sums[n % 4] + weight[n] * s
        resp_ref[at, :] = (sums[0] + sums[1]) + (sums[2] + sums[3])
        return (k, k1, v, v1, tuple(moved))

    carry = (
        shifted_start(k_ref, tail_k_ref, 1, segment),
        shifted_start(k_ref, tail_k_ref, 2, segment),
        shifted_start(v_ref, tail_v_ref, 1, segment),
        shifted_start(v_ref, tail_v_ref, 2, segment),
        (zero,) * modes,
    )
    state = lax.fori_loop(0, segment, step, carry, unroll=4)[4]
    for n in range(modes):
        end = wide(scale_ref[n : n + 1, :]) * state[n]
        rows = slice(n * SEGMENTS, (n + 1) * SEGMENTS)
        ends_ref[rows, :] = end
        last_ref[n : n + 1, :] = jnp.sum(end * reach_ref[rows, :], axis=0, keepdims=True)


def gate_kernel(
    segment, modes, parts, q_ref, tail_q_ref, taps_q_ref, lam_ref, hop_ref, residue_ref, resp_ref, ends_ref,
    states_ref, shares_ref, gated_ref, enter_ref, wide_ref,
):
    now = shares_ref[0:modes, :] * states_ref[0:modes, :]
    for i in range(1, parts):
        rows = slice(i * modes, (i + 1) * modes)
        now = now + shares_ref[rows, :] * states_ref[rows, :]
    hop = hop_ref[...]
    for s in range(SEGMENTS):
        at = pl.ds(s, modes, stride=SEGMENTS)
        enter_ref[at, :] = now
        now = hop * now + ends_ref[at, :]
    lam = [wide(lam_ref[n : n + 1, :]) for n in range(modes)]
    taps = [wide(taps_q_ref[i : i + 1, :]) for i in range(3)]
    carried = tuple(
        wide(residue_ref[n : n + 1, :]) * lam[n] * enter_ref[n * SEGMENTS : (n + 1) * SEGMENTS, :]
        for n in range(modes)
    )

    def step(t, carry):
        q1, q2, carried = carry
        at = pl.ds(t, SEGMENTS, stride=segment)
        q = q_ref[at, :]
        sums = [resp_ref[at, :], carried[0], carried[1], carried[2]]
        for n in range(3, modes):
            sums[n % 4] = sums[n % 4] + carried[n]
        response = (sums[0] + sums[1]) + (sums[2] + sums[3])
        wide_ref[at, :] = (taps[0] * q + taps[1] * q1 + taps[2] * q2) * response
        return (q, q1, tuple(lam[n] * carried[n] for n in range(modes)))

    start = (shifted_start(q_ref, tail_q_ref, 1, segment), shifted_start(q_ref, tail_q_ref, 2, segment), carried)
    lax.fori_loop(0, segment, step, start, unroll=4)
    gated_ref[...] = wide_ref[...].astype(gated_ref.dtype)


def column(rows, first):
    return pl.BlockSpec((rows, LANES), lambda c: (0, first + c))


def local_filter(projected, tails, taps, tables):
    tokens, width = projected.shape
    blocks = width // 3 // LANES
    modes = tables["lam"].shape[0]
    flops = 0
    return pl.pallas_call(
        functools.partial(local_kernel, tokens // SEGMENTS, modes),
        grid=(blocks,),
        in_specs=[
            column(tokens, blocks),
            column(tokens, 2 * blocks),
            column(2, blocks),
            column(2, 2 * blocks),
            column(3, blocks),
            column(3, 2 * blocks),
            column(modes, 0),
            column(modes, 0),
            column(modes, 0),
            column(1, 0),
            column(modes * SEGMENTS, 0),
        ],
        out_specs=[column(tokens, 0), column(modes * SEGMENTS, 0), column(modes, 0)],
        out_shape=[
            jax.ShapeDtypeStruct((tokens, width // 3), f32),
            jax.ShapeDtypeStruct((modes * SEGMENTS, width // 3), f32),
            jax.ShapeDtypeStruct((modes, width // 3), f32),
        ],
        cost_estimate=pl.CostEstimate(flops=flops, bytes_accessed=tokens * width * 4, transcendentals=0),
        compiler_params=pltpu.CompilerParams(vmem_limit_bytes=32 * 2**20),
        name="local_filter",
    )(
        projected, projected, tails, tails, taps, taps, tables["lam"], tables["weight"], tables["scale"],
        tables["skip"], tables["reach"],
    )


def gated_signal(projected, tails, taps, tables, response, ends, states, lane):
    tokens, width = projected.shape
    modes = tables["lam"].shape[0]
    parts = states.shape[0] // modes
    flops = 0
    return pl.pallas_call(
        functools.partial(gate_kernel, tokens // SEGMENTS, modes, parts),
        grid=(1,),
        in_specs=[
            column(tokens, lane),
            column(2, lane),
            column(3, lane),
            column(modes, lane),
            column(modes, lane),
            column(modes, lane),
            column(tokens, lane),
            column(modes * SEGMENTS, lane),
            column(parts * modes, lane),
            column(parts * modes, lane),
        ],
        out_specs=column(tokens, 0),
        out_shape=jax.ShapeDtypeStruct((tokens, LANES), bf16),
        scratch_shapes=[pltpu.VMEM((modes * SEGMENTS, LANES), f32), pltpu.VMEM((tokens, LANES), f32)],
        cost_estimate=pl.CostEstimate(flops=flops, bytes_accessed=tokens * width * 3, transcendentals=0),
        compiler_params=pltpu.CompilerParams(vmem_limit_bytes=32 * 2**20),
        name="gated_signal",
    )(
        projected, tails, taps, tables["lam"], tables["hop"], tables["residue"], response, ends, states,
        tables["shares"],
    )


def project_kernel(chunks, order_ref, all_ref, tails_ref, *refs):
    unit_refs, (inverse_ref, tail_inverse_ref, out_ref, tail_out_ref) = refs[:-4], refs[-4:]
    blocks = tails_ref.shape[0]

    def total(first_rows):
        result = None
        for unit, at, n, first, rows in chunks:
            block = all_ref[order_ref[n], :, first : first + rows]
            if first_rows:
                tail = tails_ref[order_ref[blocks + n], :, first : first + rows]
                block = jnp.concatenate([tail, block], axis=0)
            part = jnp.dot(block, unit_refs[unit][at : at + rows, :], preferred_element_type=f32)
            result = part if result is None else result + part
        return result

    @pl.when(pl.program_id(0) == 0)
    def _():
        result = total(True)
        tail_out_ref[...] = result[:TAIL] * tail_inverse_ref[...]
        out_ref[...] = result[TAIL:] * inverse_ref[...]

    @pl.when(pl.program_id(0) > 0)
    def _():
        out_ref[...] = total(False) * inverse_ref[...]


def project(everything, tails, units, order, inverse, tail_inverse):
    mp, tokens, features = everything.shape
    width = units[0].shape[1]
    tile = math.gcd(tokens, 256)
    chunks, row = [], 0
    for n, unit in enumerate(units):
        at = 0
        while at < unit.shape[0]:
            rows = min(features - row % features, unit.shape[0] - at)
            chunks.append((n, at, row // features, row % features, rows))
            at, row = at + rows, row + rows
    return pl.pallas_call(
        functools.partial(project_kernel, chunks),
        grid_spec=pltpu.PrefetchScalarGridSpec(
            num_scalar_prefetch=1,
            grid=(tokens // tile,),
            in_specs=[
                pl.BlockSpec((mp, tile, features), lambda m, order: (0, m, 0)),
                pl.BlockSpec((mp, TAIL, features), lambda m, order: (0, 0, 0)),
                *[pl.BlockSpec(memory_space=pltpu.VMEM) for _ in units],
                pl.BlockSpec((tile, 1), lambda m, order: (m, 0)),
                pl.BlockSpec((TAIL, 1), lambda m, order: (0, 0)),
            ],
            out_specs=[
                pl.BlockSpec((tile, width), lambda m, order: (m, 0)),
                pl.BlockSpec((TAIL, width), lambda m, order: (0, 0)),
            ],
        ),
        out_shape=[jax.ShapeDtypeStruct((tokens, width), f32), jax.ShapeDtypeStruct((TAIL, width), f32)],
        compiler_params=pltpu.CompilerParams(vmem_limit_bytes=40 * 2**20),
        name="project",
    )(order, everything, tails, *units, inverse, tail_inverse)


def output_kernel(chips, order_ref, half_ref, *refs):
    count = len(chips[0])
    gated_refs = refs[: count * len(chips)]
    panel_ref, base_refs, out_ref = refs[len(gated_refs)], refs[len(gated_refs) + 1 : -1], refs[-1]
    total = None
    for n, chip in enumerate(chips):
        rows = [ref[...] for ref in gated_refs[n * count : (n + 1) * count]]
        rows = jnp.concatenate(rows, axis=1) if count > 1 else rows[0]
        part = jnp.dot(rows, panel_ref[order_ref[n]], preferred_element_type=f32)
        total = part if total is None else total + part
    for base_ref in base_refs:
        total = total + base_ref[...].astype(f32)
    out_ref[...] = total.astype(out_ref.dtype)


def add_outputs(gated, order, panel, group, half, bases, dtype):
    tokens = gated[0][0].shape[0]
    share = len(gated[0]) * LANES
    chips, columns = panel.shape[0], panel.shape[2] // 2
    tile = math.gcd(tokens, 256)
    blocks = [block for chip in gated for block in chip]
    return pl.pallas_call(
        functools.partial(output_kernel, [[0] * len(chip) for chip in gated]),
        grid_spec=pltpu.PrefetchScalarGridSpec(
            num_scalar_prefetch=2,
            grid=(tokens // tile,),
            in_specs=[
                *[pl.BlockSpec((tile, LANES), lambda m, order, half: (m, 0)) for _ in blocks],
                pl.BlockSpec((chips, share, columns), lambda m, order, half: (0, group, half[0])),
                *[pl.BlockSpec((tile, columns), lambda m, order, half: (m, 0)) for _ in bases],
            ],
            out_specs=pl.BlockSpec((tile, columns), lambda m, order, half: (m, 0)),
        ),
        out_shape=jax.ShapeDtypeStruct((tokens, columns), dtype),
        cost_estimate=pl.CostEstimate(
            flops=4 * tokens * columns * len(gated) * share, bytes_accessed=4 * tokens * columns, transcendentals=0
        ),
        compiler_params=pltpu.CompilerParams(vmem_limit_bytes=32 * 2**20),
        name="add_outputs",
    )(order, half, *blocks, panel, *bases)


def core_swap(block):
    return lax.ppermute(block, "mp", swap_route(lax.axis_size("mp"), 1))


def ctx_order():
    size = lax.axis_size("ctx")
    index = jnp.arange(size)
    return lax.axis_index("ctx") ^ index if (size, lax.axis_size("mp")) == (4, 8) else index


def filter_tables(decay_rate, residue, skip_gain, tokens):
    me = lax.axis_index("ctx")
    size = lax.axis_size("ctx")
    rate = decay_rate.T
    modes, channels = rate.shape
    scale = jnp.sqrt(-jnp.expm1(-2.0 * rate))
    segment = tokens // SEGMENTS
    ahead = (SEGMENTS - 1 - jnp.arange(SEGMENTS, dtype=f32)) * segment
    reach = jnp.exp(-rate[:, None, :] * ahead[None, :, None]).reshape(modes * SEGMENTS, channels)
    index = ctx_order()
    gap = (me - 1 - index).astype(f32) * tokens
    shares = jnp.where(
        (index < me)[:, None, None], jnp.exp(-rate[None] * jnp.maximum(gap, 0.0)[:, None, None]), 0.0
    )
    first = jnp.exp(-rate * (me * tokens).astype(f32))[None]
    final_gap = (size - 1 - index).astype(f32) * tokens
    final = jnp.exp(-rate[None] * final_gap[:, None, None])
    final_first = jnp.exp(-rate * (size * tokens))[None]
    return {
        "lam": jnp.exp(-rate),
        "hop": jnp.exp(-rate * segment),
        "weight": residue.T * scale,
        "residue": residue.T,
        "scale": scale,
        "skip": skip_gain[None, :],
        "reach": reach,
        "shares": jnp.concatenate([shares, first]).reshape((size + 1) * modes, channels),
        "final": jnp.concatenate([final, final_first]),
    }


def cut(tables, start, stop):
    return {name: table[..., start:stop] for name, table in tables.items()}


def local(
    activations,
    norm_gain,
    w_in,
    tail_rows,
    short_filter,
    decay_rate,
    residue,
    skip_gain,
    state_in,
    w_out,
):
    tokens, features = activations.shape
    channels = w_in.shape[2]
    mp = lax.axis_size("mp")
    ctx = lax.axis_size("ctx")
    me = lax.axis_index("ctx")
    model_width = features * mp
    groups = 2 if channels % (2 * LANES) == 0 else 1
    share = channels // groups
    here = lax.axis_index("mp")
    chips = mp // 2
    chip, core = here // 2, here % 2
    special = (ctx, mp, groups) == (4, 8, 2)
    per = mp // ctx

    act_float = activations.astype(f32)
    scaled = (act_float * norm_gain[None, :]).astype(bf16)
    everything = lax.all_gather(scaled, "mp", axis=0)
    w_units = [w_in[:, :, g * share : (g + 1) * share].reshape(-1, 3 * share) for g in range(groups)]
    next_on = ("ctx", [(i, i + 1) for i in range(ctx - 1)])
    tails_all = lax.ppermute(scaled[-TAIL:], *next_on)[None]
    squares = jnp.sum(act_float * act_float, axis=1)[None]
    tables = filter_tables(decay_rate, residue, skip_gain, tokens)
    start_state = state_in.T
    tails_in = tail_rows.transpose(2, 0, 1).astype(f32)
    columns = w_out.shape[1] // per

    if special:
        along_x, along_y, across = (("ctx", swap_route(ctx, mask)) for mask in (1, 2, 3))
        along_z = ("mp", [(i, (i + 2) % mp) for i in range(mp)])
        others = [("mp", swap_route(mp, 2 * d)) for d in range(1, chips)]
        middle = w_in.shape[0] // 2
        own_rows = w_out.reshape(ctx, channels // ctx, -1)
        sent = [lax.dynamic_index_in_dim(own_rows, me ^ d, 0, False) for d in range(ctx)]
        near = send([(w_units[0], *along_x), (w_units[0], *along_y)])
        squares = squares + core_swap(squares)
        squares = squares + sum(lax.ppermute(squares, *route) for route in others)
        inverse = lax.rsqrt(squares[0] / model_width + 1e-06)[:, None]
        tail_inverse = lax.ppermute(inverse[-TAIL:], *next_on)
        first_near = near
        near, sent = lax.optimization_barrier(((near, sent), inverse))[0]
        far = send([(near[1][:middle], *along_x), (near[0][middle:], *along_y)])
        units = [[w_units[0], *near, *far]]
        got = send([(sent[1], *along_x), (sent[2], *along_y), (sent[3], *across)], first_near)
        by_owner = jnp.stack([sent[0], *got])
        tails_all = jnp.concatenate([tails_all, core_swap(tails_all)])
        tails_all = jnp.concatenate([tails_all, *[lax.ppermute(tails_all, *route) for route in others]])
        w_second = lax.optimization_barrier((w_units[1], (*far, *got, tails_all, tail_inverse)))[0]
        near = send([(w_second, *along_x), (w_second, *along_y)])
        order = jnp.stack([(me ^ (n // per)) * per + n % per for n in range(mp)]).astype(jnp.int32)
        order = jnp.concatenate([order, order ^ here])

        sent = [lax.dynamic_index_in_dim(by_owner, (chip ^ d) ^ me, 0, False) for d in range(chips)]
        own_row, *sent = sent
        by_chip = [lax.ppermute(block, *route) for block, route in zip(sent, others)]
        rows = jnp.stack([own_row, *by_chip])
        panel_order = jnp.stack([((chip - n) % chips) ^ chip for n in range(chips)]).astype(jnp.int32)
    else:
        units = []
        for g in range(groups):
            gathered = lax.all_gather(w_units[g], "ctx", axis=0)
            units.append([gathered[n] for n in range(ctx)])
        order = jnp.tile(jnp.arange(mp, dtype=jnp.int32), 2)
        tails_all = lax.all_gather(tails_all[0], "mp", axis=0)
        inverse = lax.rsqrt(lax.psum(squares, "mp")[0] / model_width + 1e-06)[:, None]
        tail_inverse = lax.ppermute(inverse[-TAIL:], *next_on)
        groups_of_core = [[i for i in range(mp) if i % 2 == c] for c in range(2)]
        rows = lax.all_to_all(w_out.reshape(ctx, channels // ctx, -1), "ctx", 0, 0)
        rows = rows.reshape(ctx, channels // ctx, chips // ctx, 2 * columns).swapaxes(1, 2)
        rows = rows.reshape(chips, channels // ctx, 2 * columns)
        rows = lax.all_to_all(rows, "mp", 0, 0, axis_index_groups=groups_of_core)
        panel = lax.all_gather(rows, "ctx", axis=1).reshape(chips, channels, 2 * columns)
        panel_order = jnp.arange(chips, dtype=jnp.int32)

    finals = []
    rings = []
    for g in range(groups):
        span = slice(g * share, (g + 1) * share)
        own = cut(tables, g * share, (g + 1) * share)
        taps = short_filter[:, :, span].reshape(3, 3 * share)
        if rings:
            order = lax.optimization_barrier((order, gated))[0]
        projected, before = project(everything, tails_all, units[g], order, inverse, tail_inverse)
        if special and g > 0:
            rings[0].append(send([(block, *along_z) for block in rings[0][-1]], [before]))
        tails = jnp.where(me == 0, tails_in[:, :, span].reshape(2, 3 * share), before[TAIL - 2 :])
        if special and g > 0:
            tails = lax.optimization_barrier((tails, rings[0][1]))[0]
        response, ends, last = local_filter(projected, tails, taps, own)
        if special:
            shared = lax.optimization_barrier((last, by_chip[0] if g == 0 else rings[0][2]))[0]
            arrived = [lax.ppermute(shared, *route) for route in (along_x, along_y, across)]
            if g == 0:
                near = lax.optimization_barrier((near, arrived))[0]
                arrived = lax.optimization_barrier((arrived, by_chip))[0]
                far = send([(near[1][:middle], *along_x), (near[0][middle:], *along_y)])
            else:
                arrived = lax.optimization_barrier((arrived, rings[0][3]))[0]
                panel_bottom = send([(bottom, *along_x), (bottom, *along_y)], arrived)
            lasts = jnp.stack([last, *arrived])
        else:
            lasts = lax.all_gather(last, "ctx", axis=0)
        states = jnp.concatenate([lasts, start_state[None, :, span]])
        finals.append(jnp.sum(own["final"] * states, axis=0))
        gated = [
            gated_signal(projected, tails, taps, own, response, ends, states.reshape(-1, share), lane)
            for lane in range(share // LANES)
        ]
        if special:
            blocks = [gated]
            for _ in range(chips - 2 if g == 0 else chips - 1):
                blocks.append([lax.ppermute(block, *along_z) for block in blocks[-1]])
            rings.append(blocks)
            if g == 0:
                units.append([w_second, *near, *far])
                top, bottom = rows[: chips // 2], rows[chips // 2 :]
                panel_top = send([(top, *along_x), (top, *along_y)], gated)
            else:
                panel_far = send([(panel_top[1], *along_x), (panel_bottom[0], *along_y)], blocks[1])
        else:
            gathered = [lax.all_gather(block, "mp", axis=0, axis_index_groups=groups_of_core) for block in gated]
            rings.append([[block[n] for block in gathered] for n in range(chips)])

    if special:
        panel = jnp.zeros((chips, ctx, *rows.shape[1:]), bf16)
        landed = [(0, 0, rows), (3, 0, panel_far[0]), (3, 2, panel_far[1])]
        landed += [(1 + n, 0, panel_top[n]) for n in range(2)] + [(1 + n, 2, panel_bottom[n]) for n in range(2)]
        for d, first, block in landed:
            panel = lax.dynamic_update_slice(panel, block[:, None], (first, me ^ d, 0, 0))
        panel = panel.reshape(chips, channels, 2 * columns)
    mine, other = core[None].astype(jnp.int32), (1 - core)[None].astype(jnp.int32)
    kept, given = [activations], []
    for g in range(groups):
        final = g == groups - 1
        steps = [slice(0, chips - 1), slice(chips - 1, chips)] if final else [slice(0, chips)]
        for n, step in enumerate(steps):
            dtype = bf16 if final and n == len(steps) - 1 else f32
            last_step = rings[g][step]
            if final and n == len(steps) - 1:
                last_step = lax.optimization_barrier((last_step, (kept[0], given[0])))[0]
            given = [add_outputs(last_step, panel_order[step], panel, g, other, given, dtype)]
            kept = [add_outputs(last_step, panel_order[step], panel, g, mine, kept, f32)]
    total = (kept[0] + core_swap(given[0]).astype(f32)).astype(bf16)
    return (total, jnp.concatenate(finals, axis=1).T)


def solution(mesh):
    placed = (
        P("ctx", "mp"),
        P("mp"),
        P("ctx", None, "mp"),
        P(None, "mp", None),
        P(None, None, "mp"),
        P("mp", None),
        P("mp", None),
        P("mp"),
        P("mp", None),
        P("mp", "ctx"),
    )
    return jax.shard_map(
        local,
        mesh=mesh,
        in_specs=placed,
        out_specs=(P("ctx", "mp"), P("mp", None)),
        check_vma=False,
    )
```

```python
import functools
import math

import jax
import jax.numpy as jnp
from jax import lax
from jax.experimental import pallas as pl
from jax.experimental.pallas import tpu as pltpu
from jax.sharding import PartitionSpec as P

LANES = 128
SEGMENTS = 8
TAIL = 16
f32 = jnp.float32
bf16 = jnp.bfloat16


def swap_route(size, bit):
    return [(i, i ^ bit) for i in range(size)]


def send(transfers, after=()):
    arrays = {id(array): array for array, _, _ in transfers}
    if len(after) > 0:
        tied = lax.optimization_barrier((list(arrays.values()), tuple(after)))[0]
        arrays = dict(zip(arrays, tied))
    return [lax.ppermute(arrays[id(array)], axis, route) for array, axis, route in transfers]


def shifted_start(ref, tail_ref, back, segment):
    last = ref[pl.ds(segment - back, SEGMENTS, stride=segment), :]
    rolled = pltpu.roll(last, 1, 0)
    first = lax.broadcasted_iota(jnp.int32, rolled.shape, 0) == 0
    return jnp.where(first, jnp.broadcast_to(tail_ref[2 - back : 3 - back, :], rolled.shape), rolled)


def wide(row):
    return jnp.broadcast_to(row, (SEGMENTS, row.shape[1]))


def local_kernel(
    segment, modes, k_ref, v_ref, tail_k_ref, tail_v_ref, taps_k_ref, taps_v_ref, lam_ref, weight_ref,
    scale_ref, skip_ref, reach_ref, resp_ref, ends_ref, last_ref,
):
    lam = [wide(lam_ref[n : n + 1, :]) for n in range(modes)]
    weight = [wide(weight_ref[n : n + 1, :]) for n in range(modes)]
    tk = [wide(taps_k_ref[i : i + 1, :]) for i in range(3)]
    tv = [wide(taps_v_ref[i : i + 1, :]) for i in range(3)]
    skip = wide(skip_ref[...])
    zero = jnp.zeros((SEGMENTS, LANES), f32)

    def step(t, carry):
        k1, k2, v1, v2, state = carry
        at = pl.ds(t, SEGMENTS, stride=segment)
        k = k_ref[at, :]
        v = v_ref[at, :]
        u = (tk[0] * k + tk[1] * k1 + tk[2] * k2) * (tv[0] * v + tv[1] * v1 + tv[2] * v2)
        sums = [skip * u, zero, zero, zero]
        moved = []
        for n in range(modes):
            s = lam[n] * state[n] + u
            moved.append(s)
            sums[n % 4] = sums[n % 4] + weight[n] * s
        resp_ref[at, :] = (sums[0] + sums[1]) + (sums[2] + sums[3])
        return (k, k1, v, v1, tuple(moved))

    carry = (
        shifted_start(k_ref, tail_k_ref, 1, segment),
        shifted_start(k_ref, tail_k_ref, 2, segment),
        shifted_start(v_ref, tail_v_ref, 1, segment),
        shifted_start(v_ref, tail_v_ref, 2, segment),
        (zero,) * modes,
    )
    state = lax.fori_loop(0, segment, step, carry, unroll=16)[4]
    for n in range(modes):
        end = wide(scale_ref[n : n + 1, :]) * state[n]
        rows = slice(n * SEGMENTS, (n + 1) * SEGMENTS)
        ends_ref[rows, :] = end
        last_ref[n : n + 1, :] = jnp.sum(end * reach_ref[rows, :], axis=0, keepdims=True)


def gate_kernel(
    segment, modes, parts, q_ref, tail_q_ref, taps_q_ref, lam_ref, hop_ref, residue_ref, resp_ref, ends_ref,
    states_ref, shares_ref, gated_ref, enter_ref, wide_ref,
):
    now = shares_ref[0:modes, :] * states_ref[0:modes, :]
    for i in range(1, parts):
        rows = slice(i * modes, (i + 1) * modes)
        now = now + shares_ref[rows, :] * states_ref[rows, :]
    hop = hop_ref[...]
    for s in range(SEGMENTS):
        at = pl.ds(s, modes, stride=SEGMENTS)
        enter_ref[at, :] = now
        now = hop * now + ends_ref[at, :]
    lam = [wide(lam_ref[n : n + 1, :]) for n in range(modes)]
    taps = [wide(taps_q_ref[i : i + 1, :]) for i in range(3)]
    carried = tuple(
        wide(residue_ref[n : n + 1, :]) * lam[n] * enter_ref[n * SEGMENTS : (n + 1) * SEGMENTS, :]
        for n in range(modes)
    )

    def step(t, carry):
        q1, q2, carried = carry
        at = pl.ds(t, SEGMENTS, stride=segment)
        q = q_ref[at, :]
        sums = [resp_ref[at, :], carried[0], carried[1], carried[2]]
        for n in range(3, modes):
            sums[n % 4] = sums[n % 4] + carried[n]
        response = (sums[0] + sums[1]) + (sums[2] + sums[3])
        wide_ref[at, :] = (taps[0] * q + taps[1] * q1 + taps[2] * q2) * response
        return (q, q1, tuple(lam[n] * carried[n] for n in range(modes)))

    start = (shifted_start(q_ref, tail_q_ref, 1, segment), shifted_start(q_ref, tail_q_ref, 2, segment), carried)
    lax.fori_loop(0, segment, step, start, unroll=8)
    gated_ref[...] = wide_ref[...].astype(gated_ref.dtype)


def column(rows, first):
    return pl.BlockSpec((rows, LANES), lambda c: (0, first + c))


def local_filter(projected, tails, taps, tables):
    tokens, width = projected.shape
    blocks = width // 3 // LANES
    modes = tables["lam"].shape[0]
    flops = 0
    return pl.pallas_call(
        functools.partial(local_kernel, tokens // SEGMENTS, modes),
        grid=(blocks,),
        in_specs=[
            column(tokens, blocks),
            column(tokens, 2 * blocks),
            column(2, blocks),
            column(2, 2 * blocks),
            column(3, blocks),
            column(3, 2 * blocks),
            column(modes, 0),
            column(modes, 0),
            column(modes, 0),
            column(1, 0),
            column(modes * SEGMENTS, 0),
        ],
        out_specs=[column(tokens, 0), column(modes * SEGMENTS, 0), column(modes, 0)],
        out_shape=[
            jax.ShapeDtypeStruct((tokens, width // 3), f32),
            jax.ShapeDtypeStruct((modes * SEGMENTS, width // 3), f32),
            jax.ShapeDtypeStruct((modes, width // 3), f32),
        ],
        cost_estimate=pl.CostEstimate(flops=flops, bytes_accessed=tokens * width * 4, transcendentals=0),
        compiler_params=pltpu.CompilerParams(vmem_limit_bytes=32 * 2**20),
        name="local_filter",
    )(
        projected, projected, tails, tails, taps, taps, tables["lam"], tables["weight"], tables["scale"],
        tables["skip"], tables["reach"],
    )


def gated_signal(projected, tails, taps, tables, response, ends, states, lane):
    tokens, width = projected.shape
    modes = tables["lam"].shape[0]
    parts = states.shape[0] // modes
    flops = 0
    return pl.pallas_call(
        functools.partial(gate_kernel, tokens // SEGMENTS, modes, parts),
        grid=(1,),
        in_specs=[
            column(tokens, lane),
            column(2, lane),
            column(3, lane),
            column(modes, lane),
            column(modes, lane),
            column(modes, lane),
            column(tokens, lane),
            column(modes * SEGMENTS, lane),
            column(parts * modes, lane),
            column(parts * modes, lane),
        ],
        out_specs=column(tokens, 0),
        out_shape=jax.ShapeDtypeStruct((tokens, LANES), bf16),
        scratch_shapes=[pltpu.VMEM((modes * SEGMENTS, LANES), f32), pltpu.VMEM((tokens, LANES), f32)],
        cost_estimate=pl.CostEstimate(flops=flops, bytes_accessed=tokens * width * 3, transcendentals=0),
        compiler_params=pltpu.CompilerParams(vmem_limit_bytes=32 * 2**20),
        name="gated_signal",
    )(
        projected, tails, taps, tables["lam"], tables["hop"], tables["residue"], response, ends, states,
        tables["shares"],
    )


def project_kernel(chunks, order_ref, all_ref, tails_ref, *refs):
    unit_refs, (inverse_ref, tail_inverse_ref, out_ref, tail_out_ref) = refs[:-4], refs[-4:]
    blocks = tails_ref.shape[0]

    def total(first_rows):
        result = None
        for unit, at, n, first, rows in chunks:
            block = all_ref[order_ref[n], :, first : first + rows]
            if first_rows:
                tail = tails_ref[order_ref[blocks + n], :, first : first + rows]
                block = jnp.concatenate([tail, block], axis=0)
            part = jnp.dot(block, unit_refs[unit][at : at + rows, :], preferred_element_type=f32)
            result = part if result is None else result + part
        return result

    @pl.when(pl.program_id(0) == 0)
    def _():
        result = total(True)
        tail_out_ref[...] = result[:TAIL] * tail_inverse_ref[...]
        out_ref[...] = result[TAIL:] * inverse_ref[...]

    @pl.when(pl.program_id(0) > 0)
    def _():
        out_ref[...] = total(False) * inverse_ref[...]


def project(everything, tails, units, order, inverse, tail_inverse, streamed):
    mp, tokens, features = everything.shape
    width = units[0].shape[1]
    tile = math.gcd(tokens, 256)
    chunks, row = [], 0
    for n, unit in enumerate(units):
        at = 0
        while at < unit.shape[0]:
            rows = min(features - row % features, unit.shape[0] - at)
            chunks.append((n, at, row // features, row % features, rows))
            at, row = at + rows, row + rows
    return pl.pallas_call(
        functools.partial(project_kernel, chunks),
        grid_spec=pltpu.PrefetchScalarGridSpec(
            num_scalar_prefetch=1,
            grid=(tokens // tile,),
            in_specs=[
                pl.BlockSpec((mp, tile, features), lambda m, order: (0, m, 0)),
                pl.BlockSpec((mp, TAIL, features), lambda m, order: (0, 0, 0)),
                *[
                    pl.BlockSpec(unit.shape, lambda m, order: (0, 0)) if n < streamed else pl.BlockSpec(memory_space=pltpu.VMEM)
                    for n, unit in enumerate(units)
                ],
                pl.BlockSpec((tile, 1), lambda m, order: (m, 0)),
                pl.BlockSpec((TAIL, 1), lambda m, order: (0, 0)),
            ],
            out_specs=[
                pl.BlockSpec((tile, width), lambda m, order: (m, 0)),
                pl.BlockSpec((TAIL, width), lambda m, order: (0, 0)),
            ],
        ),
        out_shape=[jax.ShapeDtypeStruct((tokens, width), f32), jax.ShapeDtypeStruct((TAIL, width), f32)],
        compiler_params=pltpu.CompilerParams(vmem_limit_bytes=(56 if streamed == len(units) else 40) * 2**20),
        name="project",
    )(order, everything, tails, *units, inverse, tail_inverse)


def output_kernel(chips, order_ref, half_ref, *refs):
    count = len(chips[0])
    gated_refs = refs[: count * len(chips)]
    panel_ref, base_refs, out_ref = refs[len(gated_refs)], refs[len(gated_refs) + 1 : -1], refs[-1]
    total = None
    for n, chip in enumerate(chips):
        rows = [ref[...] for ref in gated_refs[n * count : (n + 1) * count]]
        rows = jnp.concatenate(rows, axis=1) if count > 1 else rows[0]
        part = jnp.dot(rows, panel_ref[order_ref[n]], preferred_element_type=f32)
        total = part if total is None else total + part
    for base_ref in base_refs:
        total = total + base_ref[...].astype(f32)
    out_ref[...] = total.astype(out_ref.dtype)


def add_outputs(gated, order, panel, group, half, bases, dtype):
    tokens = gated[0][0].shape[0]
    share = len(gated[0]) * LANES
    chips, columns = panel.shape[0], panel.shape[2] // 2
    tile = math.gcd(tokens, 256)
    blocks = [block for chip in gated for block in chip]
    return pl.pallas_call(
        functools.partial(output_kernel, [[0] * len(chip) for chip in gated]),
        grid_spec=pltpu.PrefetchScalarGridSpec(
            num_scalar_prefetch=2,
            grid=(tokens // tile,),
            in_specs=[
                *[pl.BlockSpec((tile, LANES), lambda m, order, half: (m, 0)) for _ in blocks],
                pl.BlockSpec((chips, share, columns), lambda m, order, half: (0, group, half[0])),
                *[pl.BlockSpec((tile, columns), lambda m, order, half: (m, 0)) for _ in bases],
            ],
            out_specs=pl.BlockSpec((tile, columns), lambda m, order, half: (m, 0)),
        ),
        out_shape=jax.ShapeDtypeStruct((tokens, columns), dtype),
        cost_estimate=pl.CostEstimate(
            flops=4 * tokens * columns * len(gated) * share, bytes_accessed=4 * tokens * columns, transcendentals=0
        ),
        compiler_params=pltpu.CompilerParams(vmem_limit_bytes=32 * 2**20),
        name="add_outputs",
    )(order, half, *blocks, panel, *bases)


def core_swap(block):
    return lax.ppermute(block, "mp", swap_route(lax.axis_size("mp"), 1))


def ctx_order():
    size = lax.axis_size("ctx")
    index = jnp.arange(size)
    return lax.axis_index("ctx") ^ index if (size, lax.axis_size("mp")) == (4, 8) else index


def filter_tables(decay_rate, residue, skip_gain, tokens):
    me = lax.axis_index("ctx")
    size = lax.axis_size("ctx")
    rate = decay_rate.T
    modes, channels = rate.shape
    scale = jnp.sqrt(-jnp.expm1(-2.0 * rate))
    segment = tokens // SEGMENTS
    ahead = (SEGMENTS - 1 - jnp.arange(SEGMENTS, dtype=f32)) * segment
    reach = jnp.exp(-rate[:, None, :] * ahead[None, :, None]).reshape(modes * SEGMENTS, channels)
    index = ctx_order()
    gap = (me - 1 - index).astype(f32) * tokens
    shares = jnp.where(
        (index < me)[:, None, None], jnp.exp(-rate[None] * jnp.maximum(gap, 0.0)[:, None, None]), 0.0
    )
    first = jnp.exp(-rate * (me * tokens).astype(f32))[None]
    final_gap = (size - 1 - index).astype(f32) * tokens
    final = jnp.exp(-rate[None] * final_gap[:, None, None])
    final_first = jnp.exp(-rate * (size * tokens))[None]
    return {
        "lam": jnp.exp(-rate),
        "hop": jnp.exp(-rate * segment),
        "weight": residue.T * scale,
        "residue": residue.T,
        "scale": scale,
        "skip": skip_gain[None, :],
        "reach": reach,
        "shares": jnp.concatenate([shares, first]).reshape((size + 1) * modes, channels),
        "final": jnp.concatenate([final, final_first]),
    }


def cut(tables, start, stop):
    return {name: table[..., start:stop] for name, table in tables.items()}


def local(
    activations,
    norm_gain,
    w_in,
    tail_rows,
    short_filter,
    decay_rate,
    residue,
    skip_gain,
    state_in,
    w_out,
):
    tokens, features = activations.shape
    channels = w_in.shape[2]
    mp = lax.axis_size("mp")
    ctx = lax.axis_size("ctx")
    me = lax.axis_index("ctx")
    model_width = features * mp
    groups = 2 if channels % (2 * LANES) == 0 else 1
    share = channels // groups
    here = lax.axis_index("mp")
    chips = mp // 2
    chip, core = here // 2, here % 2
    special = (ctx, mp, groups) == (4, 8, 2)
    per = mp // ctx

    act_float = activations.astype(f32)
    scaled = (act_float * norm_gain[None, :]).astype(bf16)
    everything = lax.all_gather(scaled, "mp", axis=0)
    w_units = [w_in[:, :, g * share : (g + 1) * share].reshape(-1, 3 * share) for g in range(groups)]
    next_on = ("ctx", [(i, i + 1) for i in range(ctx - 1)])
    tails_all = lax.ppermute(scaled[-TAIL:], *next_on)[None]
    squares = jnp.sum(act_float * act_float, axis=1)[None]
    tables = filter_tables(decay_rate, residue, skip_gain, tokens)
    start_state = state_in.T
    tails_in = tail_rows.transpose(2, 0, 1).astype(f32)
    columns = w_out.shape[1] // per

    if special:
        along_x, along_y, across = (("ctx", swap_route(ctx, mask)) for mask in (1, 2, 3))
        along_z = ("mp", [(i, (i + 2) % mp) for i in range(mp)])
        others = [("mp", swap_route(mp, 2 * d)) for d in range(1, chips)]
        middle = w_in.shape[0] // 2
        own_rows = w_out.reshape(ctx, channels // ctx, -1)
        sent = [lax.dynamic_index_in_dim(own_rows, me ^ d, 0, False) for d in range(ctx)]
        near = send([(w_units[0], *along_x), (w_units[0], *along_y)])
        squares = squares + core_swap(squares)
        squares = squares + sum(lax.ppermute(squares, *route) for route in others)
        inverse = lax.rsqrt(squares[0] / model_width + 1e-06)[:, None]
        tail_inverse = lax.ppermute(inverse[-TAIL:], *next_on)
        first_near = near
        near, sent = lax.optimization_barrier(((near, sent), inverse))[0]
        far = send([(near[1][:middle], *along_x), (near[0][middle:], *along_y)])
        units = [[w_units[0], *near, *far]]
        got = send([(sent[1], *along_x), (sent[2], *along_y), (sent[3], *across)], first_near)
        by_owner = jnp.stack([sent[0], *got])
        tails_all = jnp.concatenate([tails_all, core_swap(tails_all)])
        tails_all = jnp.concatenate([tails_all, *[lax.ppermute(tails_all, *route) for route in others]])
        w_second = lax.optimization_barrier((w_units[1], (*far, *got, tails_all, tail_inverse)))[0]
        near = send([(w_second, *along_x), (w_second, *along_y)])
        order = jnp.stack([(me ^ (n // per)) * per + n % per for n in range(mp)]).astype(jnp.int32)
        order = jnp.concatenate([order, order ^ here])

        sent = [lax.dynamic_index_in_dim(by_owner, (chip ^ d) ^ me, 0, False) for d in range(chips)]
        own_row, *sent = sent
        by_chip = [lax.ppermute(block, *route) for block, route in zip(sent, others)]
        rows = jnp.stack([own_row, *by_chip])
        panel_order = jnp.stack([((chip - n) % chips) ^ chip for n in range(chips)]).astype(jnp.int32)
    else:
        units = []
        for g in range(groups):
            gathered = lax.all_gather(w_units[g], "ctx", axis=0)
            units.append([gathered[n] for n in range(ctx)])
        order = jnp.tile(jnp.arange(mp, dtype=jnp.int32), 2)
        tails_all = lax.all_gather(tails_all[0], "mp", axis=0)
        inverse = lax.rsqrt(lax.psum(squares, "mp")[0] / model_width + 1e-06)[:, None]
        tail_inverse = lax.ppermute(inverse[-TAIL:], *next_on)
        groups_of_core = [[i for i in range(mp) if i % 2 == c] for c in range(2)]
        rows = lax.all_to_all(w_out.reshape(ctx, channels // ctx, -1), "ctx", 0, 0)
        rows = rows.reshape(ctx, channels // ctx, chips // ctx, 2 * columns).swapaxes(1, 2)
        rows = rows.reshape(chips, channels // ctx, 2 * columns)
        rows = lax.all_to_all(rows, "mp", 0, 0, axis_index_groups=groups_of_core)
        panel = lax.all_gather(rows, "ctx", axis=1).reshape(chips, channels, 2 * columns)
        panel_order = jnp.arange(chips, dtype=jnp.int32)

    finals = []
    rings = []
    for g in range(groups):
        span = slice(g * share, (g + 1) * share)
        own = cut(tables, g * share, (g + 1) * share)
        taps = short_filter[:, :, span].reshape(3, 3 * share)
        if rings:
            order = lax.optimization_barrier((order, gated))[0]
        projected, before = project(everything, tails_all, units[g], order, inverse, tail_inverse, len(units[g]) if g == 0 else 1)
        if special and g > 0:
            rings[0].append(send([(block, *along_z) for block in rings[0][-1]], [before]))
        tails = jnp.where(me == 0, tails_in[:, :, span].reshape(2, 3 * share), before[TAIL - 2 :])
        if special and g > 0:
            tails = lax.optimization_barrier((tails, (*rings[0][1], *panel_top)))[0]
        response, ends, last = local_filter(projected, tails, taps, own)
        if special:
            shared = lax.optimization_barrier((last, by_chip[0] if g == 0 else rings[0][2]))[0]
            arrived = [lax.ppermute(shared, *route) for route in (along_x, along_y, across)]
            if g == 0:
                near = lax.optimization_barrier((near, arrived))[0]
                arrived = lax.optimization_barrier((arrived, by_chip))[0]
                far = send([(near[1][:middle], *along_x), (near[0][middle:], *along_y)])
            else:
                arrived = lax.optimization_barrier((arrived, rings[0][3]))[0]
                panel_bottom = send([(bottom, *along_x), (bottom, *along_y)], arrived)
            lasts = jnp.stack([last, *arrived])
        else:
            lasts = lax.all_gather(last, "ctx", axis=0)
        states = jnp.concatenate([lasts, start_state[None, :, span]])
        finals.append(jnp.sum(own["final"] * states, axis=0))
        gated = [
            gated_signal(projected, tails, taps, own, response, ends, states.reshape(-1, share), lane)
            for lane in range(share // LANES)
        ]
        if special:
            blocks = [gated]
            for _ in range(chips - 2 if g == 0 else chips - 1):
                blocks.append([lax.ppermute(block, *along_z) for block in blocks[-1]])
            rings.append(blocks)
            if g == 0:
                units.append([w_second, *near, *far])
                top, bottom = rows[: chips // 2], rows[chips // 2 :]
                panel_top = send([(top, *along_x), (top, *along_y)], gated)
            else:
                panel_far = send([(panel_top[1], *along_x), (panel_bottom[0], *along_y)], [*blocks[1][:1], panel_bottom[1]])
        else:
            gathered = [lax.all_gather(block, "mp", axis=0, axis_index_groups=groups_of_core) for block in gated]
            rings.append([[block[n] for block in gathered] for n in range(chips)])

    if special:
        panel = jnp.zeros((chips, ctx, *rows.shape[1:]), bf16)
        landed = [(0, 0, rows), (3, 0, panel_far[0]), (3, 2, panel_far[1])]
        landed += [(1 + n, 0, panel_top[n]) for n in range(2)] + [(1 + n, 2, panel_bottom[n]) for n in range(2)]
        for d, first, block in landed:
            panel = lax.dynamic_update_slice(panel, block[:, None], (first, me ^ d, 0, 0))
        panel = panel.reshape(chips, channels, 2 * columns)
    mine, other = core[None].astype(jnp.int32), (1 - core)[None].astype(jnp.int32)
    kept, given = [activations], []
    for g in range(groups - 1):
        kept = [add_outputs(rings[g], panel_order, panel, g, mine, kept, f32)]
    for g in range(groups - 1):
        given = [add_outputs(rings[g], panel_order, panel, g, other, given, f32)]
    given = [add_outputs(rings[-1][:-1], panel_order[:-1], panel, groups - 1, other, given, f32)]
    rings[-1][-1] = lax.optimization_barrier((rings[-1][-1], (kept, given)))[0]
    given = [add_outputs(rings[-1][-1:], panel_order[-1:], panel, groups - 1, other, given, bf16)]
    kept = [add_outputs(rings[-1], panel_order, panel, groups - 1, mine, kept, f32)]
    total = (kept[0] + core_swap(given[0]).astype(f32)).astype(bf16)
    return (total, jnp.concatenate(finals, axis=1).T)


def solution(mesh):
    placed = (
        P("ctx", "mp"),
        P("mp"),
        P("ctx", None, "mp"),
        P(None, "mp", None),
        P(None, None, "mp"),
        P("mp", None),
        P("mp", None),
        P("mp"),
        P("mp", None),
        P("mp", "ctx"),
    )
    return jax.shard_map(
        local,
        mesh=mesh,
        in_specs=placed,
        out_specs=(P("ctx", "mp"), P("mp", None)),
        check_vma=False,
    )
```

```python
import functools
import math

import jax
import jax.numpy as jnp
from jax import lax
from jax.experimental import pallas as pl
from jax.experimental.pallas import tpu as pltpu
from jax.sharding import PartitionSpec as P

LANES = 128
SEGMENTS = 8
TAIL = 16
f32 = jnp.float32
bf16 = jnp.bfloat16


def swap_route(size, bit):
    return [(i, i ^ bit) for i in range(size)]


def send(transfers, after=()):
    arrays = {id(array): array for array, _, _ in transfers}
    if len(after) > 0:
        tied = lax.optimization_barrier((list(arrays.values()), tuple(after)))[0]
        arrays = dict(zip(arrays, tied))
    return [lax.ppermute(arrays[id(array)], axis, route) for array, axis, route in transfers]


def shifted_start(ref, tail_ref, back, segment):
    last = ref[pl.ds(segment - back, SEGMENTS, stride=segment), :]
    rolled = pltpu.roll(last, 1, 0)
    first = lax.broadcasted_iota(jnp.int32, rolled.shape, 0) == 0
    return jnp.where(first, jnp.broadcast_to(tail_ref[2 - back : 3 - back, :], rolled.shape), rolled)


def wide(row):
    return jnp.broadcast_to(row, (SEGMENTS, row.shape[1]))


def local_kernel(
    segment, modes, k_ref, v_ref, tail_k_ref, tail_v_ref, taps_k_ref, taps_v_ref, lam_ref, weight_ref,
    scale_ref, skip_ref, reach_ref, resp_ref, ends_ref, last_ref,
):
    lam = [wide(lam_ref[n : n + 1, :]) for n in range(modes)]
    weight = [wide(weight_ref[n : n + 1, :]) for n in range(modes)]
    tk = [wide(taps_k_ref[i : i + 1, :]) for i in range(3)]
    tv = [wide(taps_v_ref[i : i + 1, :]) for i in range(3)]
    skip = wide(skip_ref[...])
    zero = jnp.zeros((SEGMENTS, LANES), f32)

    def step(t, carry):
        k1, k2, v1, v2, state = carry
        at = pl.ds(t, SEGMENTS, stride=segment)
        k = k_ref[at, :]
        v = v_ref[at, :]
        u = (tk[0] * k + tk[1] * k1 + tk[2] * k2) * (tv[0] * v + tv[1] * v1 + tv[2] * v2)
        sums = [skip * u, zero, zero, zero]
        moved = []
        for n in range(modes):
            s = lam[n] * state[n] + u
            moved.append(s)
            sums[n % 4] = sums[n % 4] + weight[n] * s
        resp_ref[at, :] = (sums[0] + sums[1]) + (sums[2] + sums[3])
        return (k, k1, v, v1, tuple(moved))

    carry = (
        shifted_start(k_ref, tail_k_ref, 1, segment),
        shifted_start(k_ref, tail_k_ref, 2, segment),
        shifted_start(v_ref, tail_v_ref, 1, segment),
        shifted_start(v_ref, tail_v_ref, 2, segment),
        (zero,) * modes,
    )
    state = lax.fori_loop(0, segment, step, carry, unroll=16)[4]
    for n in range(modes):
        end = wide(scale_ref[n : n + 1, :]) * state[n]
        rows = slice(n * SEGMENTS, (n + 1) * SEGMENTS)
        ends_ref[rows, :] = end
        last_ref[n : n + 1, :] = jnp.sum(end * reach_ref[rows, :], axis=0, keepdims=True)


def gate_kernel(
    segment, modes, parts, q_ref, tail_q_ref, taps_q_ref, lam_ref, hop_ref, residue_ref, resp_ref, ends_ref,
    states_ref, shares_ref, gated_ref, enter_ref, wide_ref,
):
    now = shares_ref[0:modes, :] * states_ref[0:modes, :]
    for i in range(1, parts):
        rows = slice(i * modes, (i + 1) * modes)
        now = now + shares_ref[rows, :] * states_ref[rows, :]
    hop = hop_ref[...]
    for s in range(SEGMENTS):
        at = pl.ds(s, modes, stride=SEGMENTS)
        enter_ref[at, :] = now
        now = hop * now + ends_ref[at, :]
    lam = [wide(lam_ref[n : n + 1, :]) for n in range(modes)]
    taps = [wide(taps_q_ref[i : i + 1, :]) for i in range(3)]
    carried = tuple(
        wide(residue_ref[n : n + 1, :]) * lam[n] * enter_ref[n * SEGMENTS : (n + 1) * SEGMENTS, :]
        for n in range(modes)
    )

    def step(t, carry):
        q1, q2, carried = carry
        at = pl.ds(t, SEGMENTS, stride=segment)
        q = q_ref[at, :]
        sums = [resp_ref[at, :], carried[0], carried[1], carried[2]]
        for n in range(3, modes):
            sums[n % 4] = sums[n % 4] + carried[n]
        response = (sums[0] + sums[1]) + (sums[2] + sums[3])
        wide_ref[at, :] = (taps[0] * q + taps[1] * q1 + taps[2] * q2) * response
        return (q, q1, tuple(lam[n] * carried[n] for n in range(modes)))

    start = (shifted_start(q_ref, tail_q_ref, 1, segment), shifted_start(q_ref, tail_q_ref, 2, segment), carried)
    lax.fori_loop(0, segment, step, start, unroll=8)
    gated_ref[...] = wide_ref[...].astype(gated_ref.dtype)


def column(rows, first):
    return pl.BlockSpec((rows, LANES), lambda c: (0, first + c))


def local_filter(projected, tails, taps, tables):
    tokens, width = projected.shape
    blocks = width // 3 // LANES
    modes = tables["lam"].shape[0]
    flops = 0
    return pl.pallas_call(
        functools.partial(local_kernel, tokens // SEGMENTS, modes),
        grid=(blocks,),
        in_specs=[
            column(tokens, blocks),
            column(tokens, 2 * blocks),
            column(2, blocks),
            column(2, 2 * blocks),
            column(3, blocks),
            column(3, 2 * blocks),
            column(modes, 0),
            column(modes, 0),
            column(modes, 0),
            column(1, 0),
            column(modes * SEGMENTS, 0),
        ],
        out_specs=[column(tokens, 0), column(modes * SEGMENTS, 0), column(modes, 0)],
        out_shape=[
            jax.ShapeDtypeStruct((tokens, width // 3), f32),
            jax.ShapeDtypeStruct((modes * SEGMENTS, width // 3), f32),
            jax.ShapeDtypeStruct((modes, width // 3), f32),
        ],
        cost_estimate=pl.CostEstimate(flops=flops, bytes_accessed=tokens * width * 4, transcendentals=0),
        compiler_params=pltpu.CompilerParams(vmem_limit_bytes=32 * 2**20),
        name="local_filter",
    )(
        projected, projected, tails, tails, taps, taps, tables["lam"], tables["weight"], tables["scale"],
        tables["skip"], tables["reach"],
    )


def gated_signal(projected, tails, taps, tables, response, ends, states, lane):
    tokens, width = projected.shape
    modes = tables["lam"].shape[0]
    parts = states.shape[0] // modes
    flops = 0
    return pl.pallas_call(
        functools.partial(gate_kernel, tokens // SEGMENTS, modes, parts),
        grid=(1,),
        in_specs=[
            column(tokens, lane),
            column(2, lane),
            column(3, lane),
            column(modes, lane),
            column(modes, lane),
            column(modes, lane),
            column(tokens, lane),
            column(modes * SEGMENTS, lane),
            column(parts * modes, lane),
            column(parts * modes, lane),
        ],
        out_specs=column(tokens, 0),
        out_shape=jax.ShapeDtypeStruct((tokens, LANES), bf16),
        scratch_shapes=[pltpu.VMEM((modes * SEGMENTS, LANES), f32), pltpu.VMEM((tokens, LANES), f32)],
        cost_estimate=pl.CostEstimate(flops=flops, bytes_accessed=tokens * width * 3, transcendentals=0),
        compiler_params=pltpu.CompilerParams(vmem_limit_bytes=32 * 2**20),
        name="gated_signal",
    )(
        projected, tails, taps, tables["lam"], tables["hop"], tables["residue"], response, ends, states,
        tables["shares"],
    )


def project_kernel(chunks, order_ref, all_ref, tails_ref, *refs):
    unit_refs, (inverse_ref, tail_inverse_ref, out_ref, tail_out_ref) = refs[:-4], refs[-4:]
    blocks = tails_ref.shape[0]

    def total(first_rows):
        result = None
        for unit, at, n, first, rows in chunks:
            block = all_ref[order_ref[n], :, first : first + rows]
            if first_rows:
                tail = tails_ref[order_ref[blocks + n], :, first : first + rows]
                block = jnp.concatenate([tail, block], axis=0)
            part = jnp.dot(block, unit_refs[unit][at : at + rows, :], preferred_element_type=f32)
            result = part if result is None else result + part
        return result

    @pl.when(pl.program_id(0) == 0)
    def _():
        result = total(True)
        tail_out_ref[...] = result[:TAIL] * tail_inverse_ref[...]
        out_ref[...] = result[TAIL:] * inverse_ref[...]

    @pl.when(pl.program_id(0) > 0)
    def _():
        out_ref[...] = total(False) * inverse_ref[...]


def project(everything, tails, units, order, inverse, tail_inverse, streamed):
    mp, tokens, features = everything.shape
    width = units[0].shape[1]
    tile = math.gcd(tokens, 256)
    chunks, row = [], 0
    for n, unit in enumerate(units):
        at = 0
        while at < unit.shape[0]:
            rows = min(features - row % features, unit.shape[0] - at)
            chunks.append((n, at, row // features, row % features, rows))
            at, row = at + rows, row + rows
    return pl.pallas_call(
        functools.partial(project_kernel, chunks),
        grid_spec=pltpu.PrefetchScalarGridSpec(
            num_scalar_prefetch=1,
            grid=(tokens // tile,),
            in_specs=[
                pl.BlockSpec((mp, tile, features), lambda m, order: (0, m, 0)),
                pl.BlockSpec((mp, TAIL, features), lambda m, order: (0, 0, 0)),
                *[
                    pl.BlockSpec(unit.shape, lambda m, order: (0, 0)) if n < streamed else pl.BlockSpec(memory_space=pltpu.VMEM)
                    for n, unit in enumerate(units)
                ],
                pl.BlockSpec((tile, 1), lambda m, order: (m, 0)),
                pl.BlockSpec((TAIL, 1), lambda m, order: (0, 0)),
            ],
            out_specs=[
                pl.BlockSpec((tile, width), lambda m, order: (m, 0)),
                pl.BlockSpec((TAIL, width), lambda m, order: (0, 0)),
            ],
        ),
        out_shape=[jax.ShapeDtypeStruct((tokens, width), f32), jax.ShapeDtypeStruct((TAIL, width), f32)],
        compiler_params=pltpu.CompilerParams(vmem_limit_bytes=(56 if streamed == len(units) else 40) * 2**20),
        name="project",
    )(order, everything, tails, *units, inverse, tail_inverse)


def output_kernel(chips, order_ref, half_ref, *refs):
    count = len(chips[0])
    gated_refs = refs[: count * len(chips)]
    panel_ref, base_refs, out_ref = refs[len(gated_refs)], refs[len(gated_refs) + 1 : -1], refs[-1]
    total = None
    for n, chip in enumerate(chips):
        rows = [ref[...] for ref in gated_refs[n * count : (n + 1) * count]]
        rows = jnp.concatenate(rows, axis=1) if count > 1 else rows[0]
        part = jnp.dot(rows, panel_ref[order_ref[n]], preferred_element_type=f32)
        total = part if total is None else total + part
    for base_ref in base_refs:
        total = total + base_ref[...].astype(f32)
    out_ref[...] = total.astype(out_ref.dtype)


def add_outputs(gated, order, panel, group, half, bases, dtype):
    tokens = gated[0][0].shape[0]
    share = len(gated[0]) * LANES
    chips, columns = panel.shape[0], panel.shape[2] // 2
    tile = math.gcd(tokens, 256)
    blocks = [block for chip in gated for block in chip]
    return pl.pallas_call(
        functools.partial(output_kernel, [[0] * len(chip) for chip in gated]),
        grid_spec=pltpu.PrefetchScalarGridSpec(
            num_scalar_prefetch=2,
            grid=(tokens // tile,),
            in_specs=[
                *[pl.BlockSpec((tile, LANES), lambda m, order, half: (m, 0)) for _ in blocks],
                pl.BlockSpec((chips, share, columns), lambda m, order, half: (0, group, half[0])),
                *[pl.BlockSpec((tile, columns), lambda m, order, half: (m, 0)) for _ in bases],
            ],
            out_specs=pl.BlockSpec((tile, columns), lambda m, order, half: (m, 0)),
        ),
        out_shape=jax.ShapeDtypeStruct((tokens, columns), dtype),
        cost_estimate=pl.CostEstimate(
            flops=4 * tokens * columns * len(gated) * share, bytes_accessed=4 * tokens * columns, transcendentals=0
        ),
        compiler_params=pltpu.CompilerParams(vmem_limit_bytes=32 * 2**20),
        name="add_outputs",
    )(order, half, *blocks, panel, *bases)


def core_swap(block):
    return lax.ppermute(block, "mp", swap_route(lax.axis_size("mp"), 1))


def ctx_order():
    size = lax.axis_size("ctx")
    index = jnp.arange(size)
    return lax.axis_index("ctx") ^ index if (size, lax.axis_size("mp")) == (4, 8) else index


def filter_tables(decay_rate, residue, skip_gain, tokens):
    me = lax.axis_index("ctx")
    size = lax.axis_size("ctx")
    rate = decay_rate.T
    modes, channels = rate.shape
    scale = jnp.sqrt(-jnp.expm1(-2.0 * rate))
    segment = tokens // SEGMENTS
    ahead = (SEGMENTS - 1 - jnp.arange(SEGMENTS, dtype=f32)) * segment
    reach = jnp.exp(-rate[:, None, :] * ahead[None, :, None]).reshape(modes * SEGMENTS, channels)
    index = ctx_order()
    gap = (me - 1 - index).astype(f32) * tokens
    shares = jnp.where(
        (index < me)[:, None, None], jnp.exp(-rate[None] * jnp.maximum(gap, 0.0)[:, None, None]), 0.0
    )
    first = jnp.exp(-rate * (me * tokens).astype(f32))[None]
    final_gap = (size - 1 - index).astype(f32) * tokens
    final = jnp.exp(-rate[None] * final_gap[:, None, None])
    final_first = jnp.exp(-rate * (size * tokens))[None]
    return {
        "lam": jnp.exp(-rate),
        "hop": jnp.exp(-rate * segment),
        "weight": residue.T * scale,
        "residue": residue.T,
        "scale": scale,
        "skip": skip_gain[None, :],
        "reach": reach,
        "shares": jnp.concatenate([shares, first]).reshape((size + 1) * modes, channels),
        "final": jnp.concatenate([final, final_first]),
    }


def cut(tables, start, stop):
    return {name: table[..., start:stop] for name, table in tables.items()}


def local(
    activations,
    norm_gain,
    w_in,
    tail_rows,
    short_filter,
    decay_rate,
    residue,
    skip_gain,
    state_in,
    w_out,
):
    tokens, features = activations.shape
    channels = w_in.shape[2]
    mp = lax.axis_size("mp")
    ctx = lax.axis_size("ctx")
    me = lax.axis_index("ctx")
    model_width = features * mp
    groups = 2 if channels % (2 * LANES) == 0 else 1
    share = channels // groups
    here = lax.axis_index("mp")
    chips = mp // 2
    chip, core = here // 2, here % 2
    special = (ctx, mp, groups) == (4, 8, 2)
    per = mp // ctx

    act_float = activations.astype(f32)
    scaled = (act_float * norm_gain[None, :]).astype(bf16)
    everything = lax.all_gather(scaled, "mp", axis=0)
    w_units = [w_in[:, :, g * share : (g + 1) * share].reshape(-1, 3 * share) for g in range(groups)]
    next_on = ("ctx", [(i, i + 1) for i in range(ctx - 1)])
    tails_all = lax.ppermute(scaled[-TAIL:], *next_on)[None]
    squares = jnp.sum(act_float * act_float, axis=1)[None]
    tables = filter_tables(decay_rate, residue, skip_gain, tokens)
    start_state = state_in.T
    tails_in = tail_rows.transpose(2, 0, 1).astype(f32)
    columns = w_out.shape[1] // per

    if special:
        along_x, along_y, across = (("ctx", swap_route(ctx, mask)) for mask in (1, 2, 3))
        along_z = ("mp", [(i, (i + 2) % mp) for i in range(mp)])
        others = [("mp", swap_route(mp, 2 * d)) for d in range(1, chips)]
        middle = w_in.shape[0] // 2
        own_rows = w_out.reshape(ctx, channels // ctx, -1)
        sent = [lax.dynamic_index_in_dim(own_rows, me ^ d, 0, False) for d in range(ctx)]
        near = send([(w_units[0], *along_x), (w_units[0], *along_y)])
        squares = squares + core_swap(squares)
        squares = squares + sum(lax.ppermute(squares, *route) for route in others)
        inverse = lax.rsqrt(squares[0] / model_width + 1e-06)[:, None]
        tail_inverse = lax.ppermute(inverse[-TAIL:], *next_on)
        first_near = near
        opposite = send([(sent[3], *across)], [squares])
        near, sent = lax.optimization_barrier(((near, sent), (inverse, opposite)))[0]
        far = send([(near[1][:middle], *along_x), (near[0][middle:], *along_y)])
        units = [[w_units[0], *near, *far]]
        got = send([(sent[1], *along_x), (sent[2], *along_y)], first_near) + opposite
        by_owner = jnp.stack([sent[0], *got])
        tails_all = jnp.concatenate([tails_all, core_swap(tails_all)])
        tails_all = jnp.concatenate([tails_all, *[lax.ppermute(tails_all, *route) for route in others]])
        second = lax.optimization_barrier((w_in, inverse))[0][:, :, share:].reshape(-1, 3 * share)
        w_second = lax.optimization_barrier((second, (*far, *got, tails_all, tail_inverse)))[0]
        near = send([(w_second, *along_x), (w_second, *along_y)])
        order = jnp.stack([(me ^ (n // per)) * per + n % per for n in range(mp)]).astype(jnp.int32)
        order = jnp.concatenate([order, order ^ here])

        sent = [lax.dynamic_index_in_dim(by_owner, (chip ^ d) ^ me, 0, False) for d in range(chips)]
        own_row, *sent = sent
        by_chip = [lax.ppermute(block, *route) for block, route in zip(sent, others)]
        rows = jnp.stack([own_row, *by_chip])
        panel_order = jnp.stack([((chip - n) % chips) ^ chip for n in range(chips)]).astype(jnp.int32)
    else:
        units = []
        for g in range(groups):
            gathered = lax.all_gather(w_units[g], "ctx", axis=0)
            units.append([gathered[n] for n in range(ctx)])
        order = jnp.tile(jnp.arange(mp, dtype=jnp.int32), 2)
        tails_all = lax.all_gather(tails_all[0], "mp", axis=0)
        inverse = lax.rsqrt(lax.psum(squares, "mp")[0] / model_width + 1e-06)[:, None]
        tail_inverse = lax.ppermute(inverse[-TAIL:], *next_on)
        groups_of_core = [[i for i in range(mp) if i % 2 == c] for c in range(2)]
        rows = lax.all_to_all(w_out.reshape(ctx, channels // ctx, -1), "ctx", 0, 0)
        rows = rows.reshape(ctx, channels // ctx, chips // ctx, 2 * columns).swapaxes(1, 2)
        rows = rows.reshape(chips, channels // ctx, 2 * columns)
        rows = lax.all_to_all(rows, "mp", 0, 0, axis_index_groups=groups_of_core)
        panel = lax.all_gather(rows, "ctx", axis=1).reshape(chips, channels, 2 * columns)
        panel_order = jnp.arange(chips, dtype=jnp.int32)

    finals = []
    rings = []
    for g in range(groups):
        span = slice(g * share, (g + 1) * share)
        own = cut(tables, g * share, (g + 1) * share)
        taps = short_filter[:, :, span].reshape(3, 3 * share)
        if rings:
            order = lax.optimization_barrier((order, gated))[0]
        projected, before = project(everything, tails_all, units[g], order, inverse, tail_inverse, len(units[g]) if g == 0 else 1)
        if special and g > 0:
            rings[0].append(send([(block, *along_z) for block in rings[0][-1]], [before]))
        tails = jnp.where(me == 0, tails_in[:, :, span].reshape(2, 3 * share), before[TAIL - 2 :])
        if special and g > 0:
            tails = lax.optimization_barrier((tails, (*rings[0][1], *panel_top)))[0]
        response, ends, last = local_filter(projected, tails, taps, own)
        if special:
            shared = lax.optimization_barrier((last, by_chip[0] if g == 0 else rings[0][2]))[0]
            arrived = [lax.ppermute(shared, *route) for route in (along_x, along_y, across)]
            if g == 0:
                near = lax.optimization_barrier((near, arrived))[0]
                arrived = lax.optimization_barrier((arrived, by_chip))[0]
                far = send([(near[1][:middle], *along_x), (near[0][middle:], *along_y)])
            else:
                arrived = lax.optimization_barrier((arrived, rings[0][3]))[0]
                panel_bottom = send([(bottom, *along_x), (bottom, *along_y)], arrived)
            lasts = jnp.stack([last, *arrived])
        else:
            lasts = lax.all_gather(last, "ctx", axis=0)
        states = jnp.concatenate([lasts, start_state[None, :, span]])
        finals.append(jnp.sum(own["final"] * states, axis=0))
        gated = [
            gated_signal(projected, tails, taps, own, response, ends, states.reshape(-1, share), lane)
            for lane in range(share // LANES)
        ]
        if special:
            blocks = [gated]
            for _ in range(chips - 2 if g == 0 else chips - 1):
                blocks.append([lax.ppermute(block, *along_z) for block in blocks[-1]])
            rings.append(blocks)
            if g == 0:
                units.append([w_second, *near, *far])
                top, bottom = rows[: chips // 2], rows[chips // 2 :]
                panel_top = send([(top, *along_x), (top, *along_y)], gated)
            else:
                panel_far = send([(panel_top[1], *along_x), (panel_bottom[0], *along_y)], [*blocks[1][:1], panel_bottom[1]])
        else:
            gathered = [lax.all_gather(block, "mp", axis=0, axis_index_groups=groups_of_core) for block in gated]
            rings.append([[block[n] for block in gathered] for n in range(chips)])

    if special:
        panel = jnp.zeros((chips, ctx, *rows.shape[1:]), bf16)
        landed = [(0, 0, rows), (3, 0, panel_far[0]), (3, 2, panel_far[1])]
        landed += [(1 + n, 0, panel_top[n]) for n in range(2)] + [(1 + n, 2, panel_bottom[n]) for n in range(2)]
        for d, first, block in landed:
            panel = lax.dynamic_update_slice(panel, block[:, None], (first, me ^ d, 0, 0))
        panel = panel.reshape(chips, channels, 2 * columns)
    mine, other = core[None].astype(jnp.int32), (1 - core)[None].astype(jnp.int32)
    kept, given = [activations], []
    for g in range(groups - 1):
        kept = [add_outputs(rings[g], panel_order, panel, g, mine, kept, f32)]
    for g in range(groups - 1):
        given = [add_outputs(rings[g], panel_order, panel, g, other, given, f32)]
    given = [add_outputs(rings[-1][:-1], panel_order[:-1], panel, groups - 1, other, given, f32)]
    rings[-1][-1] = lax.optimization_barrier((rings[-1][-1], (kept, given)))[0]
    given = [add_outputs(rings[-1][-1:], panel_order[-1:], panel, groups - 1, other, given, bf16)]
    kept = [add_outputs(rings[-1], panel_order, panel, groups - 1, mine, kept, f32)]
    total = (kept[0] + core_swap(given[0]).astype(f32)).astype(bf16)
    return (total, jnp.concatenate(finals, axis=1).T)


def solution(mesh):
    placed = (
        P("ctx", "mp"),
        P("mp"),
        P("ctx", None, "mp"),
        P(None, "mp", None),
        P(None, None, "mp"),
        P("mp", None),
        P("mp", None),
        P("mp"),
        P("mp", None),
        P("mp", "ctx"),
    )
    return jax.shard_map(
        local,
        mesh=mesh,
        in_specs=placed,
        out_specs=(P("ctx", "mp"), P("mp", None)),
        check_vma=False,
    )
```

```python
import functools
import math

import jax
import jax.numpy as jnp
from jax import lax
from jax.experimental import pallas as pl
from jax.experimental.pallas import tpu as pltpu
from jax.sharding import PartitionSpec as P

LANES = 128
SEGMENTS = 8
TAIL = 16
f32 = jnp.float32
bf16 = jnp.bfloat16


def swap_route(size, bit):
    return [(i, i ^ bit) for i in range(size)]


def send(transfers, after=()):
    arrays = {id(array): array for array, _, _ in transfers}
    if len(after) > 0:
        tied = lax.optimization_barrier((list(arrays.values()), tuple(after)))[0]
        arrays = dict(zip(arrays, tied))
    return [lax.ppermute(arrays[id(array)], axis, route) for array, axis, route in transfers]


def shifted_start(ref, tail_ref, back, segment):
    last = ref[pl.ds(segment - back, SEGMENTS, stride=segment), :]
    rolled = pltpu.roll(last, 1, 0)
    first = lax.broadcasted_iota(jnp.int32, rolled.shape, 0) == 0
    return jnp.where(first, jnp.broadcast_to(tail_ref[2 - back : 3 - back, :], rolled.shape), rolled)


def wide(row):
    return jnp.broadcast_to(row, (SEGMENTS, row.shape[1]))


def local_kernel(
    segment, modes, k_ref, v_ref, tail_k_ref, tail_v_ref, taps_k_ref, taps_v_ref, lam_ref, weight_ref,
    scale_ref, skip_ref, reach_ref, resp_ref, ends_ref, last_ref,
):
    lam = [wide(lam_ref[n : n + 1, :]) for n in range(modes)]
    weight = [wide(weight_ref[n : n + 1, :]) for n in range(modes)]
    tk = [wide(taps_k_ref[i : i + 1, :]) for i in range(3)]
    tv = [wide(taps_v_ref[i : i + 1, :]) for i in range(3)]
    skip = wide(skip_ref[...])
    zero = jnp.zeros((SEGMENTS, LANES), f32)

    def step(t, carry):
        k1, k2, v1, v2, state = carry
        at = pl.ds(t, SEGMENTS, stride=segment)
        k = k_ref[at, :]
        v = v_ref[at, :]
        u = (tk[0] * k + tk[1] * k1 + tk[2] * k2) * (tv[0] * v + tv[1] * v1 + tv[2] * v2)
        sums = [skip * u, zero, zero, zero]
        moved = []
        for n in range(modes):
            s = lam[n] * state[n] + u
            moved.append(s)
            sums[n % 4] = sums[n % 4] + weight[n] * s
        resp_ref[at, :] = (sums[0] + sums[1]) + (sums[2] + sums[3])
        return (k, k1, v, v1, tuple(moved))

    carry = (
        shifted_start(k_ref, tail_k_ref, 1, segment),
        shifted_start(k_ref, tail_k_ref, 2, segment),
        shifted_start(v_ref, tail_v_ref, 1, segment),
        shifted_start(v_ref, tail_v_ref, 2, segment),
        (zero,) * modes,
    )
    state = lax.fori_loop(0, segment, step, carry, unroll=16)[4]
    for n in range(modes):
        end = wide(scale_ref[n : n + 1, :]) * state[n]
        rows = slice(n * SEGMENTS, (n + 1) * SEGMENTS)
        ends_ref[rows, :] = end
        last_ref[n : n + 1, :] = jnp.sum(end * reach_ref[rows, :], axis=0, keepdims=True)


def gate_kernel(
    segment, modes, parts, q_ref, tail_q_ref, taps_q_ref, lam_ref, hop_ref, residue_ref, resp_ref, ends_ref,
    states_ref, shares_ref, gated_ref, enter_ref, wide_ref,
):
    now = shares_ref[0:modes, :] * states_ref[0:modes, :]
    for i in range(1, parts):
        rows = slice(i * modes, (i + 1) * modes)
        now = now + shares_ref[rows, :] * states_ref[rows, :]
    hop = hop_ref[...]
    for s in range(SEGMENTS):
        at = pl.ds(s, modes, stride=SEGMENTS)
        enter_ref[at, :] = now
        now = hop * now + ends_ref[at, :]
    lam = [wide(lam_ref[n : n + 1, :]) for n in range(modes)]
    taps = [wide(taps_q_ref[i : i + 1, :]) for i in range(3)]
    carried = tuple(
        wide(residue_ref[n : n + 1, :]) * lam[n] * enter_ref[n * SEGMENTS : (n + 1) * SEGMENTS, :]
        for n in range(modes)
    )

    def step(t, carry):
        q1, q2, carried = carry
        at = pl.ds(t, SEGMENTS, stride=segment)
        q = q_ref[at, :]
        sums = [resp_ref[at, :], carried[0], carried[1], carried[2]]
        for n in range(3, modes):
            sums[n % 4] = sums[n % 4] + carried[n]
        response = (sums[0] + sums[1]) + (sums[2] + sums[3])
        wide_ref[at, :] = (taps[0] * q + taps[1] * q1 + taps[2] * q2) * response
        return (q, q1, tuple(lam[n] * carried[n] for n in range(modes)))

    start = (shifted_start(q_ref, tail_q_ref, 1, segment), shifted_start(q_ref, tail_q_ref, 2, segment), carried)
    lax.fori_loop(0, segment, step, start, unroll=8)
    gated_ref[...] = wide_ref[...].astype(gated_ref.dtype)


def column(rows, first):
    return pl.BlockSpec((rows, LANES), lambda c: (0, first + c))


def local_filter(projected, tails, taps, tables):
    tokens, width = projected.shape
    blocks = width // 3 // LANES
    modes = tables["lam"].shape[0]
    flops = 0
    return pl.pallas_call(
        functools.partial(local_kernel, tokens // SEGMENTS, modes),
        grid=(blocks,),
        in_specs=[
            column(tokens, blocks),
            column(tokens, 2 * blocks),
            column(2, blocks),
            column(2, 2 * blocks),
            column(3, blocks),
            column(3, 2 * blocks),
            column(modes, 0),
            column(modes, 0),
            column(modes, 0),
            column(1, 0),
            column(modes * SEGMENTS, 0),
        ],
        out_specs=[column(tokens, 0), column(modes * SEGMENTS, 0), column(modes, 0)],
        out_shape=[
            jax.ShapeDtypeStruct((tokens, width // 3), f32),
            jax.ShapeDtypeStruct((modes * SEGMENTS, width // 3), f32),
            jax.ShapeDtypeStruct((modes, width // 3), f32),
        ],
        cost_estimate=pl.CostEstimate(flops=flops, bytes_accessed=tokens * width * 4, transcendentals=0),
        compiler_params=pltpu.CompilerParams(vmem_limit_bytes=32 * 2**20),
        name="local_filter",
    )(
        projected, projected, tails, tails, taps, taps, tables["lam"], tables["weight"], tables["scale"],
        tables["skip"], tables["reach"],
    )


def gated_signal(projected, tails, taps, tables, response, ends, states, lane):
    tokens, width = projected.shape
    modes = tables["lam"].shape[0]
    parts = states.shape[0] // modes
    flops = 0
    return pl.pallas_call(
        functools.partial(gate_kernel, tokens // SEGMENTS, modes, parts),
        grid=(1,),
        in_specs=[
            column(tokens, lane),
            column(2, lane),
            column(3, lane),
            column(modes, lane),
            column(modes, lane),
            column(modes, lane),
            column(tokens, lane),
            column(modes * SEGMENTS, lane),
            column(parts * modes, lane),
            column(parts * modes, lane),
        ],
        out_specs=column(tokens, 0),
        out_shape=jax.ShapeDtypeStruct((tokens, LANES), bf16),
        scratch_shapes=[pltpu.VMEM((modes * SEGMENTS, LANES), f32), pltpu.VMEM((tokens, LANES), f32)],
        cost_estimate=pl.CostEstimate(flops=flops, bytes_accessed=tokens * width * 3, transcendentals=0),
        compiler_params=pltpu.CompilerParams(vmem_limit_bytes=32 * 2**20),
        name="gated_signal",
    )(
        projected, tails, taps, tables["lam"], tables["hop"], tables["residue"], response, ends, states,
        tables["shares"],
    )


def project_kernel(chunks, order_ref, all_ref, tails_ref, *refs):
    unit_refs, (inverse_ref, tail_inverse_ref, out_ref, tail_out_ref) = refs[:-4], refs[-4:]
    blocks = tails_ref.shape[0]

    def total(first_rows):
        result = None
        for unit, at, n, first, rows in chunks:
            block = all_ref[order_ref[n], :, first : first + rows]
            if first_rows:
                tail = tails_ref[order_ref[blocks + n], :, first : first + rows]
                block = jnp.concatenate([tail, block], axis=0)
            part = jnp.dot(block, unit_refs[unit][at : at + rows, :], preferred_element_type=f32)
            result = part if result is None else result + part
        return result

    @pl.when(pl.program_id(0) == 0)
    def _():
        result = total(True)
        tail_out_ref[...] = result[:TAIL] * tail_inverse_ref[...]
        out_ref[...] = result[TAIL:] * inverse_ref[...]

    @pl.when(pl.program_id(0) > 0)
    def _():
        out_ref[...] = total(False) * inverse_ref[...]


def project(everything, tails, units, order, inverse, tail_inverse, streamed):
    mp, tokens, features = everything.shape
    width = units[0].shape[1]
    tile = math.gcd(tokens, 256)
    chunks, row = [], 0
    for n, unit in enumerate(units):
        at = 0
        while at < unit.shape[0]:
            rows = min(features - row % features, unit.shape[0] - at)
            chunks.append((n, at, row // features, row % features, rows))
            at, row = at + rows, row + rows
    return pl.pallas_call(
        functools.partial(project_kernel, chunks),
        grid_spec=pltpu.PrefetchScalarGridSpec(
            num_scalar_prefetch=1,
            grid=(tokens // tile,),
            in_specs=[
                pl.BlockSpec((mp, tile, features), lambda m, order: (0, m, 0)),
                pl.BlockSpec((mp, TAIL, features), lambda m, order: (0, 0, 0)),
                *[
                    pl.BlockSpec(unit.shape, lambda m, order: (0, 0)) if n < streamed else pl.BlockSpec(memory_space=pltpu.VMEM)
                    for n, unit in enumerate(units)
                ],
                pl.BlockSpec((tile, 1), lambda m, order: (m, 0)),
                pl.BlockSpec((TAIL, 1), lambda m, order: (0, 0)),
            ],
            out_specs=[
                pl.BlockSpec((tile, width), lambda m, order: (m, 0)),
                pl.BlockSpec((TAIL, width), lambda m, order: (0, 0)),
            ],
        ),
        out_shape=[jax.ShapeDtypeStruct((tokens, width), f32), jax.ShapeDtypeStruct((TAIL, width), f32)],
        compiler_params=pltpu.CompilerParams(vmem_limit_bytes=(56 if streamed == len(units) else 40) * 2**20),
        name="project",
    )(order, everything, tails, *units, inverse, tail_inverse)


def output_kernel(chips, order_ref, half_ref, *refs):
    count = len(chips[0])
    gated_refs = refs[: count * len(chips)]
    panel_ref, base_refs, out_ref = refs[len(gated_refs)], refs[len(gated_refs) + 1 : -1], refs[-1]
    total = None
    for n, chip in enumerate(chips):
        rows = [ref[...] for ref in gated_refs[n * count : (n + 1) * count]]
        rows = jnp.concatenate(rows, axis=1) if count > 1 else rows[0]
        part = jnp.dot(rows, panel_ref[order_ref[n]], preferred_element_type=f32)
        total = part if total is None else total + part
    for base_ref in base_refs:
        total = total + base_ref[...].astype(f32)
    out_ref[...] = total.astype(out_ref.dtype)


def add_outputs(gated, order, panel, group, half, bases, dtype):
    tokens = gated[0][0].shape[0]
    share = len(gated[0]) * LANES
    chips, columns = panel.shape[0], panel.shape[2] // 2
    tile = math.gcd(tokens, 512)
    blocks = [block for chip in gated for block in chip]
    return pl.pallas_call(
        functools.partial(output_kernel, [[0] * len(chip) for chip in gated]),
        grid_spec=pltpu.PrefetchScalarGridSpec(
            num_scalar_prefetch=2,
            grid=(tokens // tile,),
            in_specs=[
                *[pl.BlockSpec((tile, LANES), lambda m, order, half: (m, 0)) for _ in blocks],
                pl.BlockSpec((chips, share, columns), lambda m, order, half: (0, group, half[0])),
                *[pl.BlockSpec((tile, columns), lambda m, order, half: (m, 0)) for _ in bases],
            ],
            out_specs=pl.BlockSpec((tile, columns), lambda m, order, half: (m, 0)),
        ),
        out_shape=jax.ShapeDtypeStruct((tokens, columns), dtype),
        cost_estimate=pl.CostEstimate(
            flops=4 * tokens * columns * len(gated) * share, bytes_accessed=4 * tokens * columns, transcendentals=0
        ),
        compiler_params=pltpu.CompilerParams(vmem_limit_bytes=32 * 2**20),
        name="add_outputs",
    )(order, half, *blocks, panel, *bases)


def core_swap(block):
    return lax.ppermute(block, "mp", swap_route(lax.axis_size("mp"), 1))


def ctx_order():
    size = lax.axis_size("ctx")
    index = jnp.arange(size)
    return lax.axis_index("ctx") ^ index if (size, lax.axis_size("mp")) == (4, 8) else index


def filter_tables(decay_rate, residue, skip_gain, tokens):
    me = lax.axis_index("ctx")
    size = lax.axis_size("ctx")
    rate = decay_rate.T
    modes, channels = rate.shape
    scale = jnp.sqrt(-jnp.expm1(-2.0 * rate))
    segment = tokens // SEGMENTS
    ahead = (SEGMENTS - 1 - jnp.arange(SEGMENTS, dtype=f32)) * segment
    reach = jnp.exp(-rate[:, None, :] * ahead[None, :, None]).reshape(modes * SEGMENTS, channels)
    index = ctx_order()
    gap = (me - 1 - index).astype(f32) * tokens
    shares = jnp.where(
        (index < me)[:, None, None], jnp.exp(-rate[None] * jnp.maximum(gap, 0.0)[:, None, None]), 0.0
    )
    first = jnp.exp(-rate * (me * tokens).astype(f32))[None]
    final_gap = (size - 1 - index).astype(f32) * tokens
    final = jnp.exp(-rate[None] * final_gap[:, None, None])
    final_first = jnp.exp(-rate * (size * tokens))[None]
    return {
        "lam": jnp.exp(-rate),
        "hop": jnp.exp(-rate * segment),
        "weight": residue.T * scale,
        "residue": residue.T,
        "scale": scale,
        "skip": skip_gain[None, :],
        "reach": reach,
        "shares": jnp.concatenate([shares, first]).reshape((size + 1) * modes, channels),
        "final": jnp.concatenate([final, final_first]),
    }


def cut(tables, start, stop):
    return {name: table[..., start:stop] for name, table in tables.items()}


def local(
    activations,
    norm_gain,
    w_in,
    tail_rows,
    short_filter,
    decay_rate,
    residue,
    skip_gain,
    state_in,
    w_out,
):
    tokens, features = activations.shape
    channels = w_in.shape[2]
    mp = lax.axis_size("mp")
    ctx = lax.axis_size("ctx")
    me = lax.axis_index("ctx")
    model_width = features * mp
    groups = 2 if channels % (2 * LANES) == 0 else 1
    share = channels // groups
    here = lax.axis_index("mp")
    chips = mp // 2
    chip, core = here // 2, here % 2
    special = (ctx, mp, groups) == (4, 8, 2)
    per = mp // ctx

    act_float = activations.astype(f32)
    scaled = (act_float * norm_gain[None, :]).astype(bf16)
    everything = lax.all_gather(scaled, "mp", axis=0)
    w_units = [w_in[:, :, g * share : (g + 1) * share].reshape(-1, 3 * share) for g in range(groups)]
    next_on = ("ctx", [(i, i + 1) for i in range(ctx - 1)])
    tails_all = lax.ppermute(scaled[-TAIL:], *next_on)[None]
    squares = jnp.sum(act_float * act_float, axis=1)[None]
    tables = filter_tables(decay_rate, residue, skip_gain, tokens)
    start_state = state_in.T
    tails_in = tail_rows.transpose(2, 0, 1).astype(f32)
    columns = w_out.shape[1] // per

    if special:
        along_x, along_y, across = (("ctx", swap_route(ctx, mask)) for mask in (1, 2, 3))
        along_z = ("mp", [(i, (i + 2) % mp) for i in range(mp)])
        others = [("mp", swap_route(mp, 2 * d)) for d in range(1, chips)]
        middle = w_in.shape[0] // 2
        own_rows = w_out.reshape(ctx, channels // ctx, -1)
        sent = [lax.dynamic_index_in_dim(own_rows, me ^ d, 0, False) for d in range(ctx)]
        near = send([(w_units[0], *along_x), (w_units[0], *along_y)])
        squares = squares + core_swap(squares)
        squares = squares + sum(lax.ppermute(squares, *route) for route in others)
        inverse = lax.rsqrt(squares[0] / model_width + 1e-06)[:, None]
        tail_inverse = lax.ppermute(inverse[-TAIL:], *next_on)
        first_near = near
        opposite = send([(sent[3], *across)], [squares])
        near, sent = lax.optimization_barrier(((near, sent), (inverse, opposite)))[0]
        far = send([(near[1][:middle], *along_x), (near[0][middle:], *along_y)])
        units = [[w_units[0], *near, *far]]
        got = send([(sent[1], *along_x), (sent[2], *along_y)], first_near) + opposite
        by_owner = jnp.stack([sent[0], *got])
        tails_all = jnp.concatenate([tails_all, core_swap(tails_all)])
        tails_all = jnp.concatenate([tails_all, *[lax.ppermute(tails_all, *route) for route in others]])
        second = lax.optimization_barrier((w_in, inverse))[0][:, :, share:].reshape(-1, 3 * share)
        w_second = lax.optimization_barrier((second, (*far, *got, tails_all, tail_inverse)))[0]
        near = send([(w_second, *along_x), (w_second, *along_y)])
        order = jnp.stack([(me ^ (n // per)) * per + n % per for n in range(mp)]).astype(jnp.int32)
        order = jnp.concatenate([order, order ^ here])

        sent = [lax.dynamic_index_in_dim(by_owner, (chip ^ d) ^ me, 0, False) for d in range(chips)]
        own_row, *sent = sent
        by_chip = [lax.ppermute(block, *route) for block, route in zip(sent, others)]
        rows = jnp.stack([own_row, *by_chip])
        panel_order = jnp.stack([((chip - n) % chips) ^ chip for n in range(chips)]).astype(jnp.int32)
    else:
        units = []
        for g in range(groups):
            gathered = lax.all_gather(w_units[g], "ctx", axis=0)
            units.append([gathered[n] for n in range(ctx)])
        order = jnp.tile(jnp.arange(mp, dtype=jnp.int32), 2)
        tails_all = lax.all_gather(tails_all[0], "mp", axis=0)
        inverse = lax.rsqrt(lax.psum(squares, "mp")[0] / model_width + 1e-06)[:, None]
        tail_inverse = lax.ppermute(inverse[-TAIL:], *next_on)
        groups_of_core = [[i for i in range(mp) if i % 2 == c] for c in range(2)]
        rows = lax.all_to_all(w_out.reshape(ctx, channels // ctx, -1), "ctx", 0, 0)
        rows = rows.reshape(ctx, channels // ctx, chips // ctx, 2 * columns).swapaxes(1, 2)
        rows = rows.reshape(chips, channels // ctx, 2 * columns)
        rows = lax.all_to_all(rows, "mp", 0, 0, axis_index_groups=groups_of_core)
        panel = lax.all_gather(rows, "ctx", axis=1).reshape(chips, channels, 2 * columns)
        panel_order = jnp.arange(chips, dtype=jnp.int32)

    finals = []
    rings = []
    for g in range(groups):
        span = slice(g * share, (g + 1) * share)
        own = cut(tables, g * share, (g + 1) * share)
        taps = short_filter[:, :, span].reshape(3, 3 * share)
        if rings:
            order = lax.optimization_barrier((order, gated))[0]
        projected, before = project(everything, tails_all, units[g], order, inverse, tail_inverse, len(units[g]) if g == 0 else 1)
        if special and g > 0:
            rings[0].append(send([(block, *along_z) for block in rings[0][-1]], [before]))
        tails = jnp.where(me == 0, tails_in[:, :, span].reshape(2, 3 * share), before[TAIL - 2 :])
        if special and g > 0:
            tails = lax.optimization_barrier((tails, (*rings[0][1], *panel_top)))[0]
        response, ends, last = local_filter(projected, tails, taps, own)
        if special:
            shared = lax.optimization_barrier((last, by_chip[0] if g == 0 else rings[0][2]))[0]
            arrived = [lax.ppermute(shared, *route) for route in (along_x, along_y, across)]
            if g == 0:
                near = lax.optimization_barrier((near, arrived))[0]
                arrived = lax.optimization_barrier((arrived, by_chip))[0]
                far = send([(near[1][:middle], *along_x), (near[0][middle:], *along_y)])
            else:
                arrived = lax.optimization_barrier((arrived, rings[0][3]))[0]
                panel_bottom = send([(bottom, *along_x), (bottom, *along_y)], arrived)
            lasts = jnp.stack([last, *arrived])
        else:
            lasts = lax.all_gather(last, "ctx", axis=0)
        states = jnp.concatenate([lasts, start_state[None, :, span]])
        finals.append(jnp.sum(own["final"] * states, axis=0))
        gated = [
            gated_signal(projected, tails, taps, own, response, ends, states.reshape(-1, share), lane)
            for lane in range(share // LANES)
        ]
        if special:
            blocks = [gated]
            for _ in range(chips - 2 if g == 0 else chips - 1):
                blocks.append([lax.ppermute(block, *along_z) for block in blocks[-1]])
            rings.append(blocks)
            if g == 0:
                units.append([w_second, *near, *far])
                top, bottom = rows[: chips // 2], rows[chips // 2 :]
                panel_top = send([(top, *along_x), (top, *along_y)], gated)
            else:
                panel_far = send([(panel_top[1], *along_x), (panel_bottom[0], *along_y)], [*blocks[1][:1], panel_bottom[1]])
        else:
            gathered = [lax.all_gather(block, "mp", axis=0, axis_index_groups=groups_of_core) for block in gated]
            rings.append([[block[n] for block in gathered] for n in range(chips)])

    if special:
        panel = jnp.zeros((chips, ctx, *rows.shape[1:]), bf16)
        landed = [(0, 0, rows), (3, 0, panel_far[0]), (3, 2, panel_far[1])]
        landed += [(1 + n, 0, panel_top[n]) for n in range(2)] + [(1 + n, 2, panel_bottom[n]) for n in range(2)]
        for d, first, block in landed:
            panel = lax.dynamic_update_slice(panel, block[:, None], (first, me ^ d, 0, 0))
        panel = panel.reshape(chips, channels, 2 * columns)
    mine, other = core[None].astype(jnp.int32), (1 - core)[None].astype(jnp.int32)
    kept, given = [activations], []
    for g in range(groups - 1):
        kept = [add_outputs(rings[g], panel_order, panel, g, mine, kept, f32)]
    for g in range(groups - 1):
        given = [add_outputs(rings[g], panel_order, panel, g, other, given, f32)]
    given = [add_outputs(rings[-1][:-1], panel_order[:-1], panel, groups - 1, other, given, f32)]
    rings[-1][-1] = lax.optimization_barrier((rings[-1][-1], (kept, given)))[0]
    given = [add_outputs(rings[-1][-1:], panel_order[-1:], panel, groups - 1, other, given, bf16)]
    kept = [add_outputs(rings[-1], panel_order, panel, groups - 1, mine, kept, f32)]
    total = (kept[0] + core_swap(given[0]).astype(f32)).astype(bf16)
    return (total, jnp.concatenate(finals, axis=1).T)


def solution(mesh):
    placed = (
        P("ctx", "mp"),
        P("mp"),
        P("ctx", None, "mp"),
        P(None, "mp", None),
        P(None, None, "mp"),
        P("mp", None),
        P("mp", None),
        P("mp"),
        P("mp", None),
        P("mp", "ctx"),
    )
    return jax.shard_map(
        local,
        mesh=mesh,
        in_specs=placed,
        out_specs=(P("ctx", "mp"), P("mp", None)),
        check_vma=False,
    )
```
